256 devices in a mesh: lm: 32 (over x, y, core), gnn: 8 (over z).
Axes of the slice: x: 4, y: 4, z: 8, core: 2. Of those that a mesh axis runs over, the one named last changes fastest.
Arguments:
- node_states: bfloat16 [32768, 1024], P(('lm', 'gnn')), may hold values from -6 to 6
- norm_gain: float32 [1024], replicated, may hold values from 0.5 to 1.5
- w_in: bfloat16 [4096, 1024], P('lm'), may hold values from -0.1875 to 0.1875
- w_out: bfloat16 [4096, 1024], P('lm'), may hold values from -0.09375 to 0.09375
- self_one: bfloat16 [1024, 1024], P('gnn'), may hold values from -0.1875 to 0.1875
- neigh_one: bfloat16 [1024, 1024], P('gnn'), may hold values from -0.1875 to 0.1875
- self_two: bfloat16 [1024, 1024], P('gnn'), may hold values from -0.1875 to 0.1875
- neigh_two: bfloat16 [1024, 1024], P('gnn'), may hold values from -0.1875 to 0.1875
- send_slots: int32 [8192, 4], P(('lm', 'gnn')), may hold values from 0 to 127
- send_counts: int32 [256, 32], P(('lm', 'gnn')), may hold values from 1 to 4, as said below
- neighbors: int32 [32768, 10], P(('lm', 'gnn')), may hold values from 0 to 127, as said below
- out_cotangent: bfloat16 [32768, 1024], P(('lm', 'gnn')), may hold values from -6 to 6, as said below
Outputs:
- node_out: bfloat16 [32768, 1024], P(('lm', 'gnn'))
- state_grad: bfloat16 [32768, 1024], P(('lm', 'gnn'))
The draws below stay inside these ranges and needn't reach their ends.
Inputs may be any that keep to these rules, and one draw needn't show every extreme that they name: `send_slots`: entry [o * 32 + w, s] names the owned row of block o that fills slot s of the message from device o to lm index w. `send_counts`: entry [o, w] is how many leading slots of the message from device o to lm index w are filled; every device fills all 4 slots of some message. `neighbors`: every entry names a filled slot of the same worker's block of 128 slots. `out_cotangent`: zero on every empty slot.
All inputs are finite; a program needn't handle non-finite values.
Results may differ from the reference program's by a relative error of at most 0.015.
Values may be sent and summed in bfloat16 or wider, within the bound.
No kernel may reach another device: no remote copies, remote signals or barrier semaphores. Data moves between devices by JAX's collectives and lax.ppermute only.
A program may use at most 128 MiB of HBM per device.

```python
import jax
import jax.numpy as jnp
from jax import lax

D = 1024
FF = 4096
OWNED = 128
SLOT_CAP = 4
FANOUT = 10
BATCH = 128
NODE_ROWS = 32768
SLOT_ROWS = 32768
N_LM = 32
N_GNN = 8
DEVICES = 256


def count_table(key):
    key = jax.random.fold_in(key, 7)
    low_key, pick_key = jax.random.split(key)
    lowest = (SLOT_CAP + 3) // 4
    drawn = jax.random.randint(low_key, (DEVICES, N_LM), lowest, SLOT_CAP + 1, dtype=jnp.int32)
    chosen = jax.random.randint(pick_key, (DEVICES, 1), 0, N_LM, dtype=jnp.int32)
    column = jnp.arange(N_LM, dtype=jnp.int32)[None, :]
    return jnp.where(column == chosen, SLOT_CAP, drawn).astype(jnp.int32)


def draw_send_counts(key, part):
    return count_table(key)


def draw_neighbors(key, part):
    counts = count_table(key)
    key = jax.random.fold_in(key, 11)
    source_key, place_key = jax.random.split(key)
    total_rows = DEVICES * BATCH
    device = (jnp.arange(total_rows, dtype=jnp.int32) // BATCH)[:, None]
    lm_index = device // N_GNN
    gnn_index = device % N_GNN
    source = jax.random.randint(source_key, (total_rows, FANOUT), 0, N_LM, dtype=jnp.int32)
    filled = counts[source * N_GNN + gnn_index, lm_index]
    within = jax.random.randint(place_key, (total_rows, FANOUT), 0, 1 << 20, dtype=jnp.int32) % filled
    return (source * SLOT_CAP + within).astype(jnp.int32)


def draw_out_cotangent(key, part):
    counts = count_table(key)
    key = jax.random.fold_in(key, 13)
    total_rows = DEVICES * BATCH
    row_index = jnp.arange(total_rows, dtype=jnp.int32)
    device = row_index // BATCH
    local = row_index % BATCH
    source = local // SLOT_CAP
    within = local % SLOT_CAP
    filled = within < counts[source * N_GNN + device % N_GNN, device // N_GNN]
    values = jnp.clip(jax.random.normal(key, (total_rows, D), jnp.float32), -6.0, 6.0)
    return jnp.where(filled[:, None], values, 0.0).astype(jnp.bfloat16)


def touch_ends(values, own_key, least, top_value):
    dims = values.shape
    place = [jax.random.randint(jax.random.fold_in(own_key, axis), (), 0, dims[axis]) for axis in range(len(dims))]
    values = values.at[tuple(place)].set(least)
    longest = dims.index(max(dims))
    place[longest] = (place[longest] + 1) % dims[longest]
    return values.at[tuple(place)].set(top_value)


def level_of(stream_key, dims, shards, smallest, largest):
    gain, own = 1.0, jax.random.fold_in(stream_key, 6)
    for dim, shards_of in shards:
        draws = jnp.exp(jax.random.uniform(jax.random.fold_in(own, dim), (shards_of,), jnp.float32, smallest / len(shards), largest / len(shards)))
        gain = gain * jnp.repeat(draws, dims[dim] // shards_of).reshape([-1 if axis == dim else 1 for axis in range(len(dims))])
    return gain


def bell_draw(key, extent, width, most, pieces=(), kind=jnp.bfloat16):
    values = jax.random.normal(key, extent, jnp.float32) * width
    if len(pieces) > 0:
        values = level_of(key, extent, pieces, -0.22, 0.18) * values
    return jnp.clip(values, min=-most, max=most).astype(kind)


def setup_inputs(seed: int = 0) -> dict:
    arg_keys = jax.random.split(jax.random.key(seed), 13)
    node_states = bell_draw(arg_keys[0], (NODE_ROWS, D), 1.0, 6.0, ((0, 256),))
    norm_gain = jnp.clip(1.0 + 0.1 * jax.random.normal(arg_keys[1], (D,), jnp.float32), 0.5, 1.5)
    w_in = bell_draw(arg_keys[2], (FF, D), D ** -0.5, 0.1875, ((0, 32),))
    w_out = bell_draw(arg_keys[3], (FF, D), FF ** -0.5, 0.09375, ((0, 32),))
    self_one = bell_draw(arg_keys[4], (D, D), D ** -0.5, 0.1875, ((0, 8),))
    neigh_one = bell_draw(arg_keys[5], (D, D), D ** -0.5, 0.1875, ((0, 8),))
    self_two = bell_draw(arg_keys[6], (D, D), D ** -0.5, 0.1875, ((0, 8),))
    neigh_two = bell_draw(arg_keys[7], (D, D), D ** -0.5, 0.1875, ((0, 8),))
    send_slots = touch_ends(jax.random.randint(arg_keys[8], (DEVICES * N_LM, SLOT_CAP), 0, OWNED), jax.random.fold_in(arg_keys[8], 1), 0, OWNED - 1).astype(jnp.int32)
    send_counts = draw_send_counts(jax.random.fold_in(arg_keys[12], 71), 0)
    neighbors = draw_neighbors(jax.random.fold_in(arg_keys[12], 71), 0)
    out_cotangent = draw_out_cotangent(jax.random.fold_in(arg_keys[12], 71), 0)
    return {"node_states": node_states, "norm_gain": norm_gain, "w_in": w_in, "w_out": w_out, "self_one": self_one, "neigh_one": neigh_one, "self_two": self_two, "neigh_two": neigh_two, "send_slots": send_slots, "send_counts": send_counts, "neighbors": neighbors, "out_cotangent": out_cotangent}


eps_norm = 1e-06
root_coef = 0.7978845608028654
cubic_coef = 0.044715

def gelu_value(values):
    inner = root_coef * (values + cubic_coef * values * values * values)
    return 0.5 * values * (1.0 + jnp.tanh(inner))

def gelu_slope(values):
    tangent = jnp.tanh(root_coef * (values + cubic_coef * values * values * values))
    return 0.5 * (1.0 + tangent) + 0.5 * values * (1.0 - tangent * tangent) * root_coef * (1.0 + 3.0 * cubic_coef * values * values)

def silu_slope(values):
    sigmoid_v = jax.nn.sigmoid(values)
    return sigmoid_v * (1.0 + values * (1.0 - sigmoid_v))

def project_rows(left_rows, weight):
    return lax.dot_general(left_rows, weight, (((1,), (1,)), ((), ())), preferred_element_type=jnp.float32)

def normalize(states, norm_gain):
    wide = states.astype(jnp.float32)
    inv_rms = lax.rsqrt(lax.optimization_barrier(jnp.mean(wide * wide, axis=-1, keepdims=True)) + eps_norm)
    return (wide, inv_rms, (wide * inv_rms * norm_gain).astype(jnp.bfloat16))

def count_matrix(neighbors, slot_total):
    marks = neighbors[:, :, None] == jnp.arange(slot_total, dtype=jnp.int32)[None, None, :]
    return lax.optimization_barrier(jnp.sum(marks.astype(jnp.float32), axis=1)).astype(jnp.bfloat16)

def reference(node_states, norm_gain, w_in, w_out, self_one, neigh_one, self_two, neigh_two, send_slots, send_counts, neighbors, out_cotangent):
    fanout = float(FANOUT)
    states = node_states.reshape(DEVICES, OWNED, D)
    slots = send_slots.reshape(DEVICES, N_LM, SLOT_CAP)
    counts = send_counts.reshape(DEVICES, N_LM)

    def encode_pack(packed):
        block_states, block_slots, block_counts = packed
        wide, inv_rms, normed = normalize(block_states, norm_gain)
        hidden_act = gelu_value(project_rows(normed, w_in)).astype(jnp.bfloat16)
        embedded = (wide + jnp.dot(hidden_act, w_out, preferred_element_type=jnp.float32)).astype(jnp.bfloat16)
        filled = jnp.arange(SLOT_CAP, dtype=jnp.int32)[None, :] < block_counts[:, None]
        picked = jnp.take(embedded, block_slots, axis=0)
        return jnp.where(filled[:, :, None], picked, jnp.zeros_like(picked))
    outgoing = lax.map(encode_pack, (states, slots, counts))
    incoming = outgoing.reshape(N_LM, N_GNN, N_LM, SLOT_CAP, D).transpose(2, 1, 0, 3, 4).reshape(DEVICES, BATCH, D)

    def graph_step(packed):
        rows_in, block_nbrs, cotangent = packed
        neighbor_counts = count_matrix(block_nbrs, BATCH)

        def collect(features):
            return (jnp.dot(neighbor_counts, features, preferred_element_type=jnp.float32) / fanout).astype(jnp.bfloat16)

        def spread(grads):
            return lax.dot_general(neighbor_counts, grads, (((0,), (0,)), ((), ())), preferred_element_type=jnp.float32) / fanout
        first_mean = collect(rows_in)
        first_pre = jnp.dot(rows_in, self_one, preferred_element_type=jnp.float32) + jnp.dot(first_mean, neigh_one, preferred_element_type=jnp.float32)
        first_out = jax.nn.silu(first_pre).astype(jnp.bfloat16)
        second_mean = collect(first_out)
        node_out = (jnp.dot(first_out, self_two, preferred_element_type=jnp.float32) + jnp.dot(second_mean, neigh_two, preferred_element_type=jnp.float32)).astype(jnp.bfloat16)
        second_mean_grad = project_rows(cotangent, neigh_two).astype(jnp.bfloat16)
        first_out_grad = project_rows(cotangent, self_two) + spread(second_mean_grad)
        first_pre_grad = (first_out_grad * silu_slope(first_pre)).astype(jnp.bfloat16)
        first_mean_grad = project_rows(first_pre_grad, neigh_one).astype(jnp.bfloat16)
        slot_grad = (project_rows(first_pre_grad, self_one) + spread(first_mean_grad)).astype(jnp.bfloat16)
        return (node_out, slot_grad)
    node_out, slot_grad = lax.map(graph_step, (incoming, neighbors.reshape(DEVICES, BATCH, FANOUT), out_cotangent.reshape(DEVICES, BATCH, D)))
    returned = slot_grad.reshape(N_LM, N_GNN, N_LM, SLOT_CAP, D).transpose(2, 1, 0, 3, 4).reshape(DEVICES, N_LM, SLOT_CAP, D)

    def owner_back(packed):
        block_states, block_back, block_slots, block_counts = packed
        wide, inv_rms, normed = normalize(block_states, norm_gain)
        hidden_pre = project_rows(normed, w_in)
        filled = jnp.arange(SLOT_CAP, dtype=jnp.int32)[None, :] < block_counts[:, None]
        hits = (block_slots.reshape(-1)[None, :] == jnp.arange(OWNED, dtype=jnp.int32)[:, None]) & filled.reshape(-1)[None, :]
        summed = jnp.dot(hits.astype(jnp.float32), block_back.reshape(-1, D).astype(jnp.float32))
        embedded_grad = summed.astype(jnp.bfloat16)
        pre_grad = (project_rows(embedded_grad, w_out) * gelu_slope(hidden_pre)).astype(jnp.bfloat16)
        normed_grad = jnp.dot(pre_grad, w_in, preferred_element_type=jnp.float32)
        scaled = normed_grad * norm_gain
        cubed = inv_rms * inv_rms * inv_rms
        result = embedded_grad.astype(jnp.float32) + inv_rms * scaled - wide * cubed * lax.optimization_barrier(jnp.mean(scaled * wide, axis=-1, keepdims=True))
        return result.astype(jnp.bfloat16)
    state_grad = lax.map(owner_back, (states, returned, slots, counts))
    return (node_out.reshape(SLOT_ROWS, D), state_grad.reshape(NODE_ROWS, D))
```

```python
import jax
import jax.numpy as jnp
from jax import lax
from jax.experimental import pallas as pl
from jax.experimental.pallas import tpu as pltpu
from jax.sharding import Mesh
from jax.sharding import PartitionSpec as P

eps_norm = 1e-06
root_coef = 0.7978845608028654
cubic_coef = 0.044715
f32 = jnp.float32
bf16 = jnp.bfloat16

direct_order = (0, 3, 1, 2)
ring_order = (0, 3, 2, 1)
chunk_rows = 256


def nt(left, right):
    return lax.dot_general(left, right, (((1,), (1,)), ((), ())), preferred_element_type=f32)


def nn(left, right):
    return jnp.dot(left, right, preferred_element_type=f32)


def vmem_call(kernel, out_shape, scratch=(), flops=0, moved=0, limit=40):
    def call(*operands):
        return pl.pallas_call(
            kernel,
            out_shape=out_shape,
            in_specs=[pl.BlockSpec(memory_space=pltpu.VMEM)] * len(operands),
            out_specs=jax.tree.map(lambda _: pl.BlockSpec(memory_space=pltpu.VMEM), out_shape),
            scratch_shapes=list(scratch),
            compiler_params=pltpu.CompilerParams(vmem_limit_bytes=limit * 1024 * 1024),
            cost_estimate=pl.CostEstimate(flops=flops, bytes_accessed=moved, transcendentals=0),
        )(*operands)

    return call


def shape_of(dims, dtype):
    return jax.ShapeDtypeStruct(dims, dtype)


def shift(values, axis, step):
    size = lax.axis_size(axis)
    pairs = [
        (a * 2 + c, ((a + (step if c == 0 else -step)) % size) * 2 + c)
        for a in range(size)
        for c in range(2)
    ]
    return lax.ppermute(values, (axis, "core"), pairs)


def swap(values):
    return lax.ppermute(values, "core", [(0, 1), (1, 0)])


def gather_plane(shard, first, second):
    near = jnp.concatenate([shard, shift(shard, first, 1)], axis=0)
    far = jnp.concatenate([shift(shard, first, -1), shift(shard, first, 2)], axis=0)
    chunks = []
    for chunk in (near, far):
        line = [chunk]
        for _ in range(3):
            line.append(shift(line[-1], second, 1))
        chunks.extend(line)
    return chunks


def out_column(index, half):
    dx, dy = direct_order[(index // 4) * 2 + half], ring_order[index % 4]
    place = direct_order.index(dy)
    return ((place // 2) * 4 + ring_order.index(dx)) * 2 + place % 2


def ff_forward(own_ref, other_ref, gain_ref, *refs):
    in_refs, out_refs = refs[:8], refs[8:16]
    partial_ref, slope_ref, normed_ref, act_ref = refs[16:]
    for part, ref in enumerate((own_ref, other_ref)):
        wide = ref[...].astype(f32)
        inv_rms = lax.rsqrt(jnp.mean(wide * wide, axis=-1, keepdims=True) + eps_norm)
        normed_ref[part * 128 : part * 128 + 128, :] = (wide * inv_rms * gain_ref[...]).astype(bf16)
    for index in range(8):
        pre = nt(normed_ref[...], in_refs[index][...])
        square = pre * pre
        tangent = jnp.tanh(root_coef * (pre + cubic_coef * square * pre))
        act = (0.5 * pre * (1.0 + tangent)).astype(bf16)
        slope = 0.5 * (1.0 + tangent) + 0.5 * pre * (1.0 - tangent * tangent) * root_coef * (
            1.0 + 3.0 * cubic_coef * square
        )
        for half in range(2):
            at = out_column(index, half) * 128
            act_ref[:, at : at + 128] = act[:, half * 128 : half * 128 + 128]
            slope_ref[:, at : at + 128] = slope[:, half * 128 : half * 128 + 128]
    for column in range(0, 1024, 256):
        total = nn(act_ref[:, 0:256], out_refs[0][:, column : column + 256])
        for index in range(1, 8):
            total += nn(
                act_ref[:, index * 256 : index * 256 + 256],
                out_refs[index][:, column : column + 256],
            )
        partial_ref[:, column : column + 256] = total


def pick_rows(own_ref, other_ref, mine_ref, theirs_ref, pick_ref, out_ref):
    own = (own_ref[...].astype(f32) + (mine_ref[0:128, :] + theirs_ref[128:256, :])).astype(bf16)
    other = (other_ref[...].astype(f32) + (mine_ref[128:256, :] + theirs_ref[0:128, :])).astype(bf16)
    picked = nn(pick_ref[:, 0:128], own) + nn(pick_ref[:, 128:256], other)
    out_ref[...] = picked.astype(bf16)


def cotangent_part(cot_ref, count_t_ref, two_ref, base_ref, mean_grad_ref):
    for g in range(8):
        both = nt(cot_ref[...], two_ref[g * 256 : g * 256 + 256, :])
        base_ref[:, g * 128 : g * 128 + 128] = both[:, 0:128]
        mean_grad_ref[:, g * 128 : g * 128 + 128] = both[:, 128:256].astype(bf16)
    base_ref[...] += nn(count_t_ref[...], mean_grad_ref[...]) / 10.0


def graph_critical(
    in_ref, count_ref, count_t_ref, one_ref, base_ref, grad_ref, out_ref, cat_ref, own_ref, mean_ref
):
    incoming = in_ref[...]
    mean = (nn(count_ref[...], incoming) / 10.0).astype(bf16)
    for g in range(8):
        cat_ref[:, g * 256 : g * 256 + 128] = incoming[:, g * 128 : g * 128 + 128]
        cat_ref[:, g * 256 + 128 : g * 256 + 256] = mean[:, g * 128 : g * 128 + 128]
    pre = nn(cat_ref[...], one_ref[...])
    sigmoid = 1.0 / (1.0 + jnp.exp(-pre))
    out_ref[...] = (pre * sigmoid).astype(bf16)
    pre_grad = (base_ref[...] * (sigmoid * (1.0 + pre * (1.0 - sigmoid)))).astype(bf16)
    for g in range(8):
        both = nt(pre_grad, one_ref[g * 256 : g * 256 + 256, :])
        own_ref[:, g * 128 : g * 128 + 128] = both[:, 0:128]
        mean_ref[:, g * 128 : g * 128 + 128] = both[:, 128:256].astype(bf16)
    spread = nn(count_t_ref[...], mean_ref[...]) / 10.0
    grad_ref[...] = (own_ref[...] + spread).astype(bf16)


def graph_output(first_ref, count_ref, two_ref, out_ref, cat_ref):
    first = first_ref[...]
    mean = (nn(count_ref[...], first) / 10.0).astype(bf16)
    for g in range(8):
        cat_ref[:, g * 256 : g * 256 + 128] = first[:, g * 128 : g * 128 + 128]
        cat_ref[:, g * 256 + 128 : g * 256 + 256] = mean[:, g * 128 : g * 128 + 128]
    out_ref[...] = nn(cat_ref[...], two_ref[...]).astype(bf16)


def ff_backward(mine_ref, theirs_ref, put_mine_ref, put_theirs_ref, slope_ref, *refs):
    in_refs, out_refs = refs[:8], refs[8:16]
    grad_ref, own_ref, other_ref, both_ref, pre_ref = refs[16:]
    summed = nn(put_mine_ref[...], mine_ref[...]) + nn(put_theirs_ref[...], theirs_ref[...])
    both_ref[...] = summed.astype(bf16)
    grad_ref[...] = both_ref[0:128, :]
    place = {out_column(index, half): (index, half) for index in range(8) for half in range(2)}
    for index in range(8):
        grown = nt(both_ref[...], out_refs[index][...])
        grown = (grown * slope_ref[:, index * 256 : index * 256 + 256]).astype(bf16)
        for half in range(2):
            into, side = place[index * 2 + half]
            at = into * 256 + side * 128
            pre_ref[:, at : at + 128] = grown[:, half * 128 : half * 128 + 128]
    for column in range(0, 1024, 256):
        total = nn(pre_ref[:, 0:256], in_refs[0][:, column : column + 256])
        for index in range(1, 8):
            total += nn(
                pre_ref[:, index * 256 : index * 256 + 256],
                in_refs[index][:, column : column + 256],
            )
        own_ref[:, column : column + 256] = total[0:128, :]
        other_ref[:, column : column + 256] = total[128:256, :]


def finish(states_ref, gain_ref, grad_ref, mine_ref, theirs_ref, out_ref):
    wide = states_ref[...].astype(f32)
    inv_rms = lax.rsqrt(jnp.mean(wide * wide, axis=-1, keepdims=True) + eps_norm)
    scaled = (mine_ref[...] + theirs_ref[...]) * gain_ref[...]
    cubed = inv_rms * inv_rms * inv_rms
    result = (
        grad_ref[...].astype(f32)
        + inv_rms * scaled
        - wide * cubed * jnp.mean(scaled * wide, axis=-1, keepdims=True)
    )
    out_ref[...] = result.astype(bf16)


def on_device(
    node_states,
    norm_gain,
    w_in,
    w_out,
    self_one,
    neigh_one,
    self_two,
    neigh_two,
    send_slots,
    send_counts,
    neighbors,
    out_cotangent,
):
    core = lax.axis_index("core")
    first_core = core == 0
    gain = norm_gain.reshape(1, 1024)

    layer_rows = jnp.where(
        first_core,
        jnp.concatenate([self_one, neigh_one], axis=0),
        jnp.concatenate([self_two, neigh_two], axis=0),
    )
    layer_mine = lax.all_gather(layer_rows, "gnn", axis=0, tiled=True)

    other_states = swap(node_states)
    in_chunks = gather_plane(w_in, "x", "y")
    out_chunks = gather_plane(w_out, "y", "x")

    filled = jnp.arange(4, dtype=jnp.int32)[None, :] < send_counts[0][:, None]
    own_ids = jnp.where(filled, send_slots, -1)
    other_ids = swap(own_ids)
    own_ids = own_ids.reshape(16, 2, 4)
    other_ids = other_ids.reshape(16, 2, 4)
    other_ids = jnp.where(other_ids < 0, -1, other_ids + 128)

    def slot_ids(worker_first):
        own = jnp.where(worker_first, own_ids[:, 0], own_ids[:, 1])
        other = jnp.where(worker_first, other_ids[:, 0], other_ids[:, 1])
        return jnp.stack(
            [jnp.where(first_core, own, other), jnp.where(first_core, other, own)], axis=1
        ).reshape(128)

    mine_ids, theirs_ids = slot_ids(first_core), slot_ids(jnp.logical_not(first_core))
    rows = jnp.arange(256, dtype=jnp.int32)
    pick_mine = (mine_ids[:, None] == rows[None, :]).astype(bf16)
    put_mine = (rows[:, None] == mine_ids[None, :]).astype(bf16)
    put_theirs = (rows[:, None] == theirs_ids[None, :]).astype(bf16)
    marks = neighbors[:, :, None] == jnp.arange(128, dtype=jnp.int32)[None, None, :]
    count = jnp.sum(marks.astype(f32), axis=1).astype(bf16)
    count_t = count.T

    partial, slope = vmem_call(
        ff_forward,
        (shape_of((256, 1024), f32), shape_of((256, 2048), f32)),
        scratch=[pltpu.VMEM((256, 1024), bf16), pltpu.VMEM((256, 2048), bf16)],
        flops=2 * 2 * 256 * 1024 * 2048,
        moved=12 << 20,
    )(node_states, other_states, gain, *in_chunks, *out_chunks)
    partial_theirs = swap(partial)
    outgoing = vmem_call(
        pick_rows, shape_of((128, 1024), bf16), flops=2 * 128 * 256 * 1024, moved=3 << 20
    )(node_states, other_states, partial, partial_theirs, pick_mine)
    incoming = lax.all_to_all(
        outgoing.reshape(16, 8, 1024), ("x", "y"), split_axis=0, concat_axis=0, tiled=True
    ).reshape(128, 1024)

    layer_theirs = swap(layer_mine)
    layer_one = jnp.where(first_core, layer_mine, layer_theirs)
    layer_two = jnp.where(first_core, layer_theirs, layer_mine)
    layer_flops = 2 * 128 * 1024 * 2048
    base = vmem_call(
        cotangent_part,
        shape_of((128, 1024), f32),
        scratch=[pltpu.VMEM((128, 1024), bf16)],
        flops=layer_flops,
        moved=5 << 20,
    )(out_cotangent, count_t, layer_two)
    slot_grad, first_out = vmem_call(
        graph_critical,
        (shape_of((128, 1024), bf16), shape_of((128, 1024), bf16)),
        scratch=[
            pltpu.VMEM((128, 2048), bf16),
            pltpu.VMEM((128, 1024), f32),
            pltpu.VMEM((128, 1024), bf16),
        ],
        flops=2 * layer_flops,
        moved=5 << 20,
    )(incoming, count, count_t, layer_one, base)
    returned = lax.all_to_all(
        slot_grad.reshape(16, 8, 1024), ("x", "y"), split_axis=0, concat_axis=0, tiled=True
    ).reshape(128, 1024)
    node_out = vmem_call(
        graph_output,
        shape_of((128, 1024), bf16),
        scratch=[pltpu.VMEM((128, 2048), bf16)],
        flops=layer_flops,
        moved=5 << 20,
    )(first_out, count, layer_two)
    returned_theirs = swap(returned)
    embedded_grad, grad_mine, grad_other = vmem_call(
        ff_backward,
        (shape_of((128, 1024), bf16), shape_of((128, 1024), f32), shape_of((128, 1024), f32)),
        scratch=[pltpu.VMEM((256, 1024), bf16), pltpu.VMEM((256, 2048), bf16)],
        flops=2 * 2 * 256 * 1024 * 2048,
        moved=12 << 20,
    )(returned, returned_theirs, put_mine, put_theirs, slope, *in_chunks, *out_chunks)
    grad_theirs = swap(grad_other)
    state_grad = vmem_call(finish, shape_of((128, 1024), bf16), moved=2 << 20)(
        node_states, gain, embedded_grad, grad_mine, grad_theirs
    )
    return node_out, state_grad


def solution(mesh):
    split = Mesh(mesh.devices.reshape(4, 4, 2, 8), ("x", "y", "core", "gnn"))
    lm, everywhere = ("x", "y", "core"), ("x", "y", "core", "gnn")
    rows, by_lm, by_gnn = P(everywhere, None), P(lm, None), P("gnn", None)
    return jax.shard_map(
        on_device,
        mesh=split,
        in_specs=(rows, P(), by_lm, by_lm, by_gnn, by_gnn, by_gnn, by_gnn, rows, rows, rows, rows),
        out_specs=(rows, rows),
        check_vma=False,
    )
```

```python
import jax
import jax.numpy as jnp
from jax import lax
from jax.experimental import pallas as pl
from jax.experimental.pallas import tpu as pltpu
from jax.sharding import Mesh
from jax.sharding import PartitionSpec as P

eps_norm = 1e-06
root_coef = 0.7978845608028654
cubic_coef = 0.044715
f32 = jnp.float32
bf16 = jnp.bfloat16

layer_order = (0, -1, 1, -2, 2, -3, 3, -4)
near_layers = 5
early_blocks = 10


def nt(left, right):
    return lax.dot_general(left, right, (((1,), (1,)), ((), ())), preferred_element_type=f32)


def nn(left, right):
    return jnp.dot(left, right, preferred_element_type=f32)


def local_call(kernel, out_shape, ins, outs, scratch=(), flops=0, moved=0, limit=10):
    specs = {
        "v": pl.BlockSpec(memory_space=pltpu.VMEM),
        "s": pl.BlockSpec(memory_space=pltpu.SMEM),
        "b": pl.BlockSpec(),
        "h": pl.BlockSpec(memory_space=pltpu.HBM),
    }
    return pl.pallas_call(
        kernel,
        out_shape=out_shape,
        in_specs=[specs[kind] for kind in ins],
        out_specs=[specs[kind] for kind in outs],
        scratch_shapes=list(scratch),
        compiler_params=pltpu.CompilerParams(vmem_limit_bytes=limit * 1024 * 1024),
        cost_estimate=pl.CostEstimate(flops=flops, bytes_accessed=moved, transcendentals=0),
    )


def shape_of(dims, dtype):
    return jax.ShapeDtypeStruct(dims, dtype)


def swap(values):
    return lax.ppermute(values, "core", [(0, 1), (1, 0)])


def shift_plane(values, phase, step):
    pairs = []
    for x in range(4):
        for y in range(4):
            for c in range(2):
                along_x = (phase == 1) == (c == 0)
                to = ((x + step) % 4, y) if along_x else (x, (y + step) % 4)
                pairs.append(((x * 4 + y) * 2 + c, (to[0] * 4 + to[1]) * 2 + c))
    return lax.ppermute(values, ("x", "y", "core"), pairs)


def shift_first(values, step):
    return shift_plane(values, 1, step)


def shift_second(values, step):
    return shift_plane(values, 2, step)


def gather_weights(block, part, states, ids):
    steps = {
        "right_1": ("part", shift_ring, 1),
        "left_1": ("part", shift_ring, -1),
        "ahead": ("block", shift_first, 1),
        "behind": ("block", shift_first, -1),
        "up_0": ("block", shift_second, 1),
        "right_2": ("right_1", shift_ring, 1, "ahead", "behind", "up_0"),
        "left_2": ("left_1", shift_ring, -1, "ahead", "behind", "up_0"),
        "opposite": ("ahead", shift_first, 1, "right_1", "left_1"),
        "down_1": ("ahead", shift_second, -1, "right_1", "left_1"),
        "up_3": ("behind", shift_second, 1, "right_1", "left_1"),
        "down_0": ("block", shift_second, -1, "opposite"),
        "up_1": ("ahead", shift_second, 1, "opposite"),
        "down_3": ("behind", shift_second, -1, "down_1"),
        "far_0": ("up_0", shift_second, 1, "up_3"),
        "states": ("states_mine", swap, 0, "opposite", "down_1", "up_3"),
        "ids": ("ids_mine", swap, 0, "opposite", "down_1", "up_3"),
        "right_3": ("right_2", shift_ring, 1, "opposite", "down_1", "up_3"),
        "left_3": ("left_2", shift_ring, -1, "opposite", "down_1", "up_3"),
        "near": (("part", "right_1", "left_1", "right_2", "left_2"), swap, 0, "opposite", "down_1", "up_3"),
        "up_2": ("opposite", shift_second, 1, "right_2", "left_2"),
        "down_2": ("opposite", shift_second, -1, "right_2", "left_2"),
        "far_1": ("down_1", shift_second, -1, "right_2", "left_2", "states", "ids", "near"),
        "right_4": ("right_3", shift_ring, 1, "up_2", "down_2", "up_1", "down_0", "near"),
        "far_3": ("up_3", shift_second, 1, "right_3", "left_3", "near"),
        "far_2": ("down_2", shift_second, -1, "right_3", "left_3", "near"),
        "far": (("right_3", "left_3", "right_4"), swap, 0),
    }
    held = {"block": block, "part": part, "states_mine": states, "ids_mine": ids}
    mine = []
    for name, (source, shift, step, *others) in steps.items():
        if isinstance(source, tuple):
            values = join_parts([held[entry] for entry in source])
            mine.append(values)
        else:
            values = held[source]
        if others:
            values, _ = lax.optimization_barrier((values, [held[entry] for entry in others]))
        held[name] = swap(values) if shift is swap else shift(values, step)
    order = (
        "block", "ahead", "behind", "up_0", "opposite", "down_1", "up_3", "down_0", "up_1",
        "down_3", "up_2", "down_2", "far_0", "far_1", "far_3", "far_2",
    )
    layers = [mine[0], held["near"], mine[1], held["far"]]
    return [held[name] for name in order], layers, held["states"], held["ids"]


def shift_ring(values, step):
    pairs = [
        (c * 8 + g, c * 8 + (g + (step if c == 0 else -step)) % 8) for c in range(2) for g in range(8)
    ]
    return lax.ppermute(values, ("core", "gnn"), pairs)


def start_copy(source, target, sem):
    copy = pltpu.make_async_copy(source, target, sem)
    copy.start()
    return copy


def prepare(in_ref, out_ref, *refs):
    block_ref, half_ref, place_ref, sems = refs[4:]
    core = lax.axis_index("core")
    columns = pl.ds(pl.multiple_of(core * 512, 512), 512)
    copies = [
        start_copy(in_ref, block_ref.at[0:128, :], sems.at[0]),
        start_copy(out_ref, block_ref.at[128:256, :], sems.at[1]),
    ]
    for index in range(4):
        target = half_ref.at[index * 128 : index * 128 + 128, :]
        copies.append(start_copy(refs[index].at[:, columns], target, sems.at[2 + index]))
    place_ref[0] = core
    place_ref[1] = lax.axis_index("gnn")
    for copy in copies:
        copy.wait()


def join(*refs):
    for index, ref in enumerate(refs[:-1]):
        refs[-1][index * 512 : index * 512 + 512, :] = ref[...]


def join_parts(parts):
    (whole,) = local_call(
        join,
        [shape_of((len(parts) * 512, 512), bf16)],
        "v" * len(parts),
        "v",
        moved=len(parts) << 20,
    )(*parts)
    return whole


def transposed(left, eye):
    return lax.dot_general(left, eye, (((0,), (0,)), ((), ())), preferred_element_type=f32)


def index_tables(place_ref, own_ref, other_ref, neighbors_ref, *refs):
    pick_mine_ref, put_mine_ref, put_theirs_ref, count_ref, count_t_ref = refs
    core = place_ref[0]

    def iota(rows, columns, axis):
        return lax.broadcasted_iota(jnp.int32, (rows, columns), axis)

    eye = (iota(128, 128, 0) == iota(128, 128, 1)).astype(bf16)
    own, other = own_ref[...].astype(f32).astype(bf16), other_ref[...].astype(f32).astype(bf16)
    slot = iota(128, 4, 0) & 3 == iota(128, 4, 1)
    side = (iota(128, 1, 0) >> 2) & 1

    def pick(worker):
        rows = (iota(128, 32, 1) == (iota(128, 32, 0) >> 3) * 2 + worker).astype(bf16)
        own_id = jnp.sum(jnp.where(slot, nt(rows, own), 0.0), axis=1, keepdims=True)
        other_id = jnp.sum(jnp.where(slot, nt(rows, other), 0.0), axis=1, keepdims=True)
        other_id = jnp.where(other_id < 0.0, -1.0, other_id + 128.0)
        ids = jnp.where(side == core, own_id, other_id).astype(jnp.int32)
        return (ids == iota(128, 256, 1)).astype(bf16)

    mine = pick(core)
    pick_mine_ref[...] = mine
    put_mine_ref[...] = transposed(mine, eye).astype(bf16)
    put_theirs_ref[...] = transposed(pick(1 - core), eye).astype(bf16)
    count_t = jnp.zeros((128, 128), f32)
    for index in range(neighbors_ref.shape[0]):
        count_t += (neighbors_ref[index : index + 1, :] == iota(128, 128, 0)).astype(f32)
    count_t = count_t.astype(bf16)
    count_t_ref[...] = count_t
    count_ref[...] = transposed(count_t, eye).astype(bf16)


def in_rows(refs, pair):
    return jnp.concatenate([refs[2 * pair][0:128, :], refs[2 * pair + 1][0:128, :]], axis=0)


def out_rows(refs, pair, column):
    at = slice(column, column + 256)
    return jnp.concatenate([refs[2 * pair][128:256, at], refs[2 * pair + 1][128:256, at]], axis=0)


def expand_blocks(normed_ref, refs, slope_ref, act_ref):
    for pair in range(len(refs) // 2):
        pre = nt(normed_ref[...], in_rows(refs, pair))
        square = pre * pre
        tangent = jnp.tanh(root_coef * (pre + cubic_coef * square * pre))
        at = slice(pair * 256, pair * 256 + 256)
        act_ref[:, at] = (0.5 * pre * (1.0 + tangent)).astype(bf16)
        slope_ref[:, at] = 0.5 * (1.0 + tangent) + 0.5 * pre * (
            1.0 - tangent * tangent
        ) * root_coef * (1.0 + 3.0 * cubic_coef * square)


def contract_blocks(act_ref, refs, column):
    total = nn(act_ref[:, 0:256], out_rows(refs, 0, column))
    for pair in range(1, len(refs) // 2):
        total += nn(act_ref[:, pair * 256 : pair * 256 + 256], out_rows(refs, pair, column))
    return total


def ff_early(own_ref, other_ref, gain_ref, *refs):
    blocks = refs[:early_blocks]
    partial_ref, slope_ref, normed_ref, act_ref = refs[-4:]
    for part, ref in enumerate((own_ref, other_ref)):
        wide = ref[...].astype(f32)
        inv_rms = lax.rsqrt(jnp.mean(wide * wide, axis=-1, keepdims=True) + eps_norm)
        normed_ref[part * 128 : part * 128 + 128, :] = (wide * inv_rms * gain_ref[...]).astype(bf16)
    expand_blocks(normed_ref, blocks, slope_ref, act_ref)
    for column in range(0, 1024, 256):
        partial_ref[:, column : column + 256] = contract_blocks(act_ref, blocks, column)


def ff_late(normed_ref, early_ref, *refs):
    blocks = refs[: 16 - early_blocks]
    partial_ref, slope_ref, act_ref = refs[-3:]
    expand_blocks(normed_ref, blocks, slope_ref, act_ref)
    for column in range(0, 1024, 256):
        at = slice(column, column + 256)
        partial_ref[:, at] = early_ref[:, at] + contract_blocks(act_ref, blocks, column)


def pick_rows(own_ref, other_ref, mine_ref, theirs_ref, pick_ref, _, out_ref):
    own = (own_ref[...].astype(f32) + (mine_ref[0:128, :] + theirs_ref[128:256, :])).astype(bf16)
    other = (other_ref[...].astype(f32) + (mine_ref[128:256, :] + theirs_ref[0:128, :])).astype(bf16)
    picked = nn(pick_ref[:, 0:128], own) + nn(pick_ref[:, 128:256], other)
    out_ref[...] = picked.astype(bf16)


def interleave(rows_ref, mean, cat_ref):
    for g in range(8):
        at = slice(g * 128, g * 128 + 128)
        cat_ref[:, g * 256 : g * 256 + 128] = rows_ref[:, at]
        cat_ref[:, g * 256 + 128 : g * 256 + 256] = mean[:, at]


def layer_backward(grad, layer_ref, own_ref, mean_ref):
    for g in range(8):
        at = slice(g * 128, g * 128 + 128)
        both = nt(grad, layer_ref[g * 256 : g * 256 + 256, :])
        own_ref[:, at] = both[:, 0:128]
        mean_ref[:, at] = both[:, 128:256].astype(bf16)


def lay_layer(place_ref, layer, near_refs, far_refs, layer_ref, sems):
    core, gnn = place_ref[0], place_ref[1]
    copies = []
    for half in range(2):
        side = core if half == 0 else 1 - core
        column = pl.multiple_of(side * 512, 512)
        for index, offset in enumerate(layer_order):
            shard = lax.rem(gnn + (1 - 2 * side) * offset + 8, 8) * 256
            ref = (near_refs if index < near_layers else far_refs)[half]
            start = (index if index < near_layers else index - near_layers) * 512 + layer * 256
            target = layer_ref.at[pl.ds(pl.multiple_of(shard, 256), 256), pl.ds(column, 512)]
            copies.append(start_copy(ref.at[start : start + 256, :], target, sems.at[half * 8 + index]))
    return copies


def cotangent_part(place_ref, cot_ref, count_t_ref, *refs):
    near_refs, far_refs = refs[0:2], refs[2:4]
    base_ref, one_ref, two_ref, mean_grad_ref, one_sems, two_sems = refs[4:]
    two_copies = lay_layer(place_ref, 1, near_refs, far_refs, two_ref, two_sems)
    one_copies = lay_layer(place_ref, 0, near_refs, far_refs, one_ref, one_sems)
    for copy in two_copies:
        copy.wait()
    layer_backward(cot_ref[...], two_ref, base_ref, mean_grad_ref)
    base_ref[...] += nn(count_t_ref[...], mean_grad_ref[...]) / 10.0
    for copy in one_copies:
        copy.wait()


def graph_critical(
    in_ref, count_ref, count_t_ref, one_ref, base_ref, grad_ref, out_ref, cat_ref, own_ref, mean_ref
):
    interleave(in_ref, (nn(count_ref[...], in_ref[...]) / 10.0).astype(bf16), cat_ref)
    pre = nn(cat_ref[...], one_ref[...])
    sigmoid = 1.0 / (1.0 + jnp.exp(-pre))
    out_ref[...] = (pre * sigmoid).astype(bf16)
    pre_grad = (base_ref[...] * (sigmoid * (1.0 + pre * (1.0 - sigmoid)))).astype(bf16)
    layer_backward(pre_grad, one_ref, own_ref, mean_ref)
    spread = nn(count_t_ref[...], mean_ref[...]) / 10.0
    grad_ref[...] = (own_ref[...] + spread).astype(bf16)


def graph_output(first_ref, count_ref, two_ref, out_ref, cat_ref):
    interleave(first_ref, (nn(count_ref[...], first_ref[...]) / 10.0).astype(bf16), cat_ref)
    out_ref[...] = nn(cat_ref[...], two_ref[...]).astype(bf16)


def ff_backward(mine_ref, theirs_ref, put_mine_ref, put_theirs_ref, *refs):
    slope_refs, blocks = refs[:2], refs[2:18]
    grad_ref, own_ref, other_ref, both_ref, pre_ref = refs[18:]
    summed = nn(put_mine_ref[...], mine_ref[...]) + nn(put_theirs_ref[...], theirs_ref[...])
    both_ref[...] = summed.astype(bf16)
    grad_ref[...] = both_ref[0:128, :]
    for pair in range(8):
        rows = jnp.concatenate([blocks[2 * pair][128:256, :], blocks[2 * pair + 1][128:256, :]], axis=0)
        late = pair >= early_blocks // 2
        start = pair * 256 - (early_blocks * 128 if late else 0)
        grown = nt(both_ref[...], rows) * slope_refs[late][:, start : start + 256]
        pre_ref[:, pair * 256 : pair * 256 + 256] = grown.astype(bf16)
    for column in range(0, 1024, 256):
        at = slice(column, column + 256)
        total = None
        for pair in range(8):
            rows = jnp.concatenate([blocks[2 * pair][0:128, at], blocks[2 * pair + 1][0:128, at]], axis=0)
            term = nn(pre_ref[:, pair * 256 : pair * 256 + 256], rows)
            total = term if total is None else total + term
        own_ref[:, at] = total[0:128, :]
        other_ref[:, at] = total[128:256, :]


def finish(states_ref, gain_ref, grad_ref, mine_ref, theirs_ref, out_ref):
    wide = states_ref[...].astype(f32)
    inv_rms = lax.rsqrt(jnp.mean(wide * wide, axis=-1, keepdims=True) + eps_norm)
    scaled = (mine_ref[...] + theirs_ref[...]) * gain_ref[...]
    cubed = inv_rms * inv_rms * inv_rms
    result = (
        grad_ref[...].astype(f32)
        + inv_rms * scaled
        - wide * cubed * jnp.mean(scaled * wide, axis=-1, keepdims=True)
    )
    out_ref[...] = result.astype(bf16)


def on_device(
    node_states,
    norm_gain,
    w_in,
    w_out,
    self_one,
    neigh_one,
    self_two,
    neigh_two,
    send_slots,
    send_counts,
    neighbors,
    out_cotangent,
):
    gain = norm_gain.reshape(1, 1024)
    block, layer_half, place = local_call(
        prepare,
        [shape_of((256, 1024), bf16), shape_of((512, 512), bf16), shape_of((2,), jnp.int32)],
        "hhhhhh",
        "vvs",
        [pltpu.SemaphoreType.DMA((6,))],
        moved=2 << 20,
        limit=60,
    )(w_in, w_out, self_one, neigh_one, self_two, neigh_two)
    filled = jnp.arange(4, dtype=jnp.int32)[None, :] < send_counts[0][:, None]
    own_ids = jnp.where(filled, send_slots, -1)
    blocks, layers, other_states, other_ids = gather_weights(block, layer_half, node_states, own_ids)
    pick_mine, put_mine, put_theirs, count, count_t = local_call(
        index_tables,
        [shape_of((128, 256), bf16)] + [shape_of((256, 128), bf16)] * 2 + [shape_of((128, 128), bf16)] * 2,
        "sbbb",
        "vvvvv",
        moved=1 << 20,
    )(place, own_ids.T, other_ids.T, neighbors.T)

    late_blocks = 16 - early_blocks
    block_flops = 2 * 2 * 256 * 1024 * 128
    early, slope_early, normed = local_call(
        ff_early,
        [
            shape_of((256, 1024), f32),
            shape_of((256, early_blocks * 128), f32),
            shape_of((256, 1024), bf16),
        ],
        "vvv" + "v" * early_blocks,
        "vvv",
        [pltpu.VMEM((256, early_blocks * 128), bf16)],
        flops=block_flops * early_blocks,
        moved=9 << 20,
    )(node_states, other_states, gain, *blocks[:early_blocks])
    partial, slope_late = local_call(
        ff_late,
        [shape_of((256, 1024), f32), shape_of((256, late_blocks * 128), f32)],
        "vv" + "v" * late_blocks,
        "vv",
        [pltpu.VMEM((256, late_blocks * 128), bf16)],
        flops=block_flops * late_blocks,
        moved=6 << 20,
    )(normed, early, *blocks[early_blocks:])
    partial_theirs = swap(partial)
    layer_flops = 2 * 128 * 1024 * 2048
    base, layer_one, layer_two = local_call(
        cotangent_part,
        [shape_of((128, 1024), f32), shape_of((2048, 1024), bf16), shape_of((2048, 1024), bf16)],
        "svv" + "v" * 4,
        "vvv",
        [pltpu.VMEM((128, 1024), bf16)] + [pltpu.SemaphoreType.DMA((16,))] * 2,
        flops=layer_flops,
        moved=18 << 20,
    )(place, out_cotangent, count_t, *layers)
    (outgoing,) = local_call(
        pick_rows,
        [shape_of((128, 1024), bf16)],
        "vvvvvv",
        "v",
        flops=2 * 128 * 256 * 1024,
        moved=3 << 20,
    )(node_states, other_states, partial, partial_theirs, pick_mine, base)
    incoming = lax.all_to_all(
        outgoing.reshape(16, 8, 1024), ("x", "y"), split_axis=0, concat_axis=0, tiled=True
    ).reshape(128, 1024)
    slot_grad, first_out = local_call(
        graph_critical,
        [shape_of((128, 1024), bf16), shape_of((128, 1024), bf16)],
        "vvvvv",
        "vv",
        [
            pltpu.VMEM((128, 2048), bf16),
            pltpu.VMEM((128, 1024), f32),
            pltpu.VMEM((128, 1024), bf16),
        ],
        flops=2 * layer_flops,
        moved=5 << 20,
    )(incoming, count, count_t, layer_one, base)
    returned = lax.all_to_all(
        slot_grad.reshape(16, 8, 1024), ("x", "y"), split_axis=0, concat_axis=0, tiled=True
    ).reshape(128, 1024)
    returned_theirs = swap(returned)
    embedded_grad, grad_mine, grad_other = local_call(
        ff_backward,
        [shape_of((128, 1024), bf16), shape_of((128, 1024), f32), shape_of((128, 1024), f32)],
        "vvvvvv" + "v" * 16,
        "vvv",
        [pltpu.VMEM((256, 1024), bf16), pltpu.VMEM((256, 2048), bf16)],
        flops=block_flops * 16,
        moved=14 << 20,
    )(returned, returned_theirs, put_mine, put_theirs, slope_early, slope_late, *blocks)
    grad_theirs = swap(grad_other)
    (node_out,) = local_call(
        graph_output,
        [shape_of((128, 1024), bf16)],
        "vvv",
        "b",
        [pltpu.VMEM((128, 2048), bf16)],
        flops=layer_flops,
        moved=5 << 20,
    )(first_out, count, layer_two)
    (state_grad,) = local_call(
        finish, [shape_of((128, 1024), bf16)], "vvvvv", "b", moved=2 << 20
    )(node_states, gain, embedded_grad, grad_mine, grad_theirs)
    return node_out, state_grad


def solution(mesh):
    split = Mesh(mesh.devices.reshape(4, 4, 2, 8), ("x", "y", "core", "gnn"))
    lm, everywhere = ("x", "y", "core"), ("x", "y", "core", "gnn")
    rows, by_lm, by_gnn = P(everywhere, None), P(lm, None), P("gnn", None)
    return jax.shard_map(
        on_device,
        mesh=split,
        in_specs=(rows, P(), by_lm, by_lm, by_gnn, by_gnn, by_gnn, by_gnn, rows, rows, rows, rows),
        out_specs=(rows, rows),
        check_vma=False,
    )
```

```python
import jax
import jax.numpy as jnp
from jax import lax
from jax.experimental import pallas as pl
from jax.experimental.pallas import tpu as pltpu
from jax.sharding import Mesh
from jax.sharding import PartitionSpec as P

eps_norm = 1e-06
root_coef = 0.7978845608028654
cubic_coef = 0.044715
f32 = jnp.float32
bf16 = jnp.bfloat16

layer_order = (0, -1, 1, -2, 2, -3, 3, -4)
early_arrays = 3
early_blocks = 12


def nt(left, right):
    return lax.dot_general(left, right, (((1,), (1,)), ((), ())), preferred_element_type=f32)


def nn(left, right):
    return jnp.dot(left, right, preferred_element_type=f32)


def local_call(kernel, out_shape, ins, outs, scratch=(), flops=0, moved=0, limit=10, aliases=None):
    specs = {
        "v": pl.BlockSpec(memory_space=pltpu.VMEM),
        "s": pl.BlockSpec(memory_space=pltpu.SMEM),
        "b": pl.BlockSpec(),
        "h": pl.BlockSpec(memory_space=pltpu.HBM),
    }
    return pl.pallas_call(
        kernel,
        out_shape=out_shape,
        in_specs=[specs[kind] for kind in ins],
        out_specs=[specs[kind] for kind in outs],
        scratch_shapes=list(scratch),
        input_output_aliases=aliases or {},
        compiler_params=pltpu.CompilerParams(vmem_limit_bytes=limit * 1024 * 1024),
        cost_estimate=pl.CostEstimate(flops=flops, bytes_accessed=moved, transcendentals=0),
    )


def shape_of(dims, dtype):
    return jax.ShapeDtypeStruct(dims, dtype)


def swap(values):
    return lax.ppermute(values, "core", [(0, 1), (1, 0)])


def shift_plane(values, phase, step):
    pairs = []
    for x in range(4):
        for y in range(4):
            for c in range(2):
                along_x = (phase == 1) == (c == 0)
                to = ((x + step) % 4, y) if along_x else (x, (y + step) % 4)
                pairs.append(((x * 4 + y) * 2 + c, (to[0] * 4 + to[1]) * 2 + c))
    return lax.ppermute(values, ("x", "y", "core"), pairs)


def shift_first(values, step):
    return shift_plane(values, 1, step)


def shift_second(values, step):
    return shift_plane(values, 2, step)


def after(values, *others):
    return lax.optimization_barrier((values, others))[0]


def gather_weights(block, part, states):
    right_1, left_1 = shift_ring(part, 1), shift_ring(part, -1)
    ahead, behind, opposite = shift_first(block, 1), shift_first(block, -1), shift_first(block, 2)
    other_states = swap(states)
    line = join_parts([block, ahead, behind, opposite])

    first = (right_1, left_1, ahead, behind, opposite, other_states)
    right_2 = shift_ring(after(right_1, first), 1)
    left_2 = shift_ring(after(left_1, first), -1)
    right_3 = shift_ring(after(right_1, first), 2)
    line = after(line, first)
    up, down = shift_second(line, 1), shift_second(line, -1)

    second = (right_2, left_2, right_3, up, down)
    left_3 = shift_ring(after(left_2, second), -1)
    right_4 = shift_ring(after(right_3, second), 1)
    far_up = shift_second(after(cut_rows(up, 0), second), 1)
    far_down = shift_second(after(cut_rows(down, 512), second), -1)
    near = join_parts(after([part, right_1, left_1, right_2, left_2, right_3], second))
    near_theirs = swap(near)

    third = (left_3, right_4, far_up, far_down, near_theirs)
    far = join_parts(after([left_3, right_4], third))
    return [line, up, down, far_up, far_down], (near, near_theirs), (far, swap(far)), other_states


def shift_ring(values, step):
    pairs = [
        (c * 8 + g, c * 8 + (g + (step if c == 0 else -step)) % 8) for c in range(2) for g in range(8)
    ]
    return lax.ppermute(values, ("core", "gnn"), pairs)


def start_copy(source, target, sem):
    copy = pltpu.make_async_copy(source, target, sem)
    copy.start()
    return copy


def prepare(in_ref, out_ref, *refs):
    block_ref, half_ref, place_ref, sems = refs[4:]
    core = lax.axis_index("core")
    columns = pl.ds(pl.multiple_of(core * 512, 512), 512)
    copies = [
        start_copy(in_ref, block_ref.at[0:128, :], sems.at[0]),
        start_copy(out_ref, block_ref.at[128:256, :], sems.at[1]),
    ]
    for index in range(4):
        target = half_ref.at[index * 128 : index * 128 + 128, :]
        copies.append(start_copy(refs[index].at[:, columns], target, sems.at[2 + index]))
    place_ref[0] = core
    place_ref[1] = lax.axis_index("gnn")
    for copy in copies:
        copy.wait()


def join(*refs):
    rows = refs[0].shape[0]
    for index, ref in enumerate(refs[:-1]):
        refs[-1][index * rows : index * rows + rows, :] = ref[...]


def pack(states_ref, ids_ref, out_ref):
    out_ref[0:128, :] = states_ref[...]
    out_ref[128:144, :] = jnp.zeros((16, 1024), bf16)
    ids = ids_ref[...].astype(f32).astype(bf16)
    rows = (lax.broadcasted_iota(jnp.int32, (16, 4), 0) == lax.broadcasted_iota(jnp.int32, (16, 4), 1)).astype(bf16)
    columns = (lax.broadcasted_iota(jnp.int32, (32, 128), 0) == lax.broadcasted_iota(jnp.int32, (32, 128), 1)).astype(bf16)
    out_ref[128:144, 0:128] = nn(nn(rows, ids).astype(bf16), columns).astype(bf16)


def join_parts(parts):
    rows, columns = parts[0].shape
    (whole,) = local_call(
        join,
        [shape_of((len(parts) * rows, columns), bf16)],
        "v" * len(parts),
        "v",
        moved=len(parts) << 20,
    )(*parts)
    return whole


def cut_rows(values, start):
    def cut(ref, out_ref):
        out_ref[...] = ref[start : start + 512, :]

    (rows,) = local_call(cut, [shape_of((512, 1024), bf16)], "v", "v", moved=2 << 20)(values)
    return rows


def transposed(left, eye):
    return lax.dot_general(left, eye, (((0,), (0,)), ((), ())), preferred_element_type=f32)


def index_tables(place_ref, own_ref, other_ref, neighbors_ref, *refs):
    pick_mine_ref, put_mine_ref, put_theirs_ref, count_ref, count_t_ref = refs
    core = place_ref[0]

    def iota(rows, columns, axis):
        return lax.broadcasted_iota(jnp.int32, (rows, columns), axis)

    eye = (iota(128, 128, 0) == iota(128, 128, 1)).astype(bf16)
    own, other = own_ref[...].astype(f32).astype(bf16), other_ref[128:144, 0:128][0:4, 0:32]
    slot = iota(128, 4, 0) & 3 == iota(128, 4, 1)
    side = (iota(128, 1, 0) >> 2) & 1

    def pick(worker):
        rows = (iota(128, 32, 1) == (iota(128, 32, 0) >> 3) * 2 + worker).astype(bf16)
        own_id = jnp.sum(jnp.where(slot, nt(rows, own), 0.0), axis=1, keepdims=True)
        other_id = jnp.sum(jnp.where(slot, nt(rows, other), 0.0), axis=1, keepdims=True)
        other_id = jnp.where(other_id < 0.0, -1.0, other_id + 128.0)
        ids = jnp.where(side == core, own_id, other_id).astype(jnp.int32)
        return (ids == iota(128, 256, 1)).astype(bf16)

    mine = pick(core)
    pick_mine_ref[...] = mine
    put_mine_ref[...] = transposed(mine, eye).astype(bf16)
    put_theirs_ref[...] = transposed(pick(1 - core), eye).astype(bf16)
    count_t = jnp.zeros((128, 128), f32)
    for index in range(neighbors_ref.shape[0]):
        count_t += (neighbors_ref[index : index + 1, :] == iota(128, 128, 0)).astype(f32)
    count_t = count_t.astype(bf16)
    count_t_ref[...] = count_t
    count_ref[...] = transposed(count_t, eye).astype(bf16)


def units(refs):
    return [(ref, start) for ref in refs for start in range(0, ref.shape[0], 256)]


def in_rows(blocks, pair, at=slice(None)):
    return jnp.concatenate([ref[s : s + 128, at] for ref, s in blocks[2 * pair : 2 * pair + 2]], axis=0)


def out_rows(blocks, pair, at=slice(None)):
    return jnp.concatenate([ref[s + 128 : s + 256, at] for ref, s in blocks[2 * pair : 2 * pair + 2]], axis=0)


def expand_blocks(normed_ref, blocks, slope_ref, act_ref):
    for pair in range(len(blocks) // 2):
        pre = nt(normed_ref[...], in_rows(blocks, pair))
        square = pre * pre
        tangent = jnp.tanh(root_coef * (pre + cubic_coef * square * pre))
        at = slice(pair * 256, pair * 256 + 256)
        act_ref[:, at] = (0.5 * pre * (1.0 + tangent)).astype(bf16)
        slope_ref[:, at] = 0.5 * (1.0 + tangent) + 0.5 * pre * (
            1.0 - tangent * tangent
        ) * root_coef * (1.0 + 3.0 * cubic_coef * square)


def contract_blocks(act_ref, blocks, at):
    total = nn(act_ref[:, 0:256], out_rows(blocks, 0, at))
    for pair in range(1, len(blocks) // 2):
        total += nn(act_ref[:, pair * 256 : pair * 256 + 256], out_rows(blocks, pair, at))
    return total


def ff_early(own_ref, other_ref, gain_ref, *refs):
    blocks = units(refs[:early_arrays])
    partial_ref, slope_ref, normed_ref, act_ref = refs[-4:]
    for part, ref in enumerate((own_ref, other_ref)):
        wide = ref[0:128, :].astype(f32)
        inv_rms = lax.rsqrt(jnp.mean(wide * wide, axis=-1, keepdims=True) + eps_norm)
        normed_ref[part * 128 : part * 128 + 128, :] = (wide * inv_rms * gain_ref[...]).astype(bf16)
    expand_blocks(normed_ref, blocks, slope_ref, act_ref)
    for column in range(0, 1024, 256):
        at = slice(column, column + 256)
        partial_ref[:, at] = contract_blocks(act_ref, blocks, at)


def ff_late(normed_ref, early_ref, *refs):
    partial_ref, slope_ref, act_ref = refs[-3:]
    blocks = units(refs[:-3])
    expand_blocks(normed_ref, blocks, slope_ref, act_ref)
    for column in range(0, 1024, 256):
        at = slice(column, column + 256)
        partial_ref[:, at] = early_ref[:, at] + contract_blocks(act_ref, blocks, at)


def pick_rows(own_ref, other_ref, mine_ref, theirs_ref, pick_ref, _, out_ref):
    own = (own_ref[...].astype(f32) + (mine_ref[0:128, :] + theirs_ref[128:256, :])).astype(bf16)
    other = (other_ref[0:128, :].astype(f32) + (mine_ref[128:256, :] + theirs_ref[0:128, :])).astype(bf16)
    picked = nn(pick_ref[:, 0:128], own) + nn(pick_ref[:, 128:256], other)
    out_ref[...] = picked.astype(bf16)


def interleave(rows_ref, mean, cat_ref):
    for g in range(8):
        at = slice(g * 128, g * 128 + 128)
        cat_ref[:, g * 256 : g * 256 + 128] = rows_ref[:, at]
        cat_ref[:, g * 256 + 128 : g * 256 + 256] = mean[:, at]


def layer_backward(grad, layer_ref, own_ref, mean_ref):
    for g in range(8):
        at = slice(g * 128, g * 128 + 128)
        both = nt(grad, layer_ref[g * 256 : g * 256 + 256, :])
        own_ref[:, at] = both[:, 0:128]
        mean_ref[:, at] = both[:, 128:256].astype(bf16)


def shard_rows(place_ref, offset):
    return pl.multiple_of(lax.rem(place_ref[1] + offset + 8, 8) * 256, 256)


def lay_layer(place_ref, layer, places, refs, layer_ref, sems):
    copies = []
    for half in range(2):
        side = place_ref[0] if half == 0 else 1 - place_ref[0]
        column = pl.multiple_of(side * 512, 512)
        for index, (array, start, offset) in enumerate(places):
            rows = pl.ds(shard_rows(place_ref, (1 - 2 * side) * offset), 256)
            start += layer * 256
            target = layer_ref.at[rows, pl.ds(column, 512)]
            source = refs[half][array].at[start : start + 256, :]
            copies.append(start_copy(source, target, sems.at[half * 5 + index]))
    return copies


def cotangent_part(place_ref, cot_ref, places, refs, outs):
    own_ref, mean_ref, one_ref, two_ref, one_sems, two_sems = outs
    two_copies = lay_layer(place_ref, 1, places, refs, two_ref, two_sems)
    one_copies = lay_layer(place_ref, 0, places, refs, one_ref, one_sems)
    for copy in two_copies:
        copy.wait()
    for _, _, offset in places:
        rows = shard_rows(place_ref, offset)
        at = pl.ds(pl.multiple_of(lax.rem(place_ref[1] + offset + 8, 8) * 128, 128), 128)
        both = nt(cot_ref[...], two_ref[pl.ds(rows, 256), :])
        own_ref[:, at] = both[:, 0:128]
        mean_ref[:, at] = both[:, 128:256].astype(bf16)
    return one_copies


def cotangent_near(place_ref, cot_ref, mine_ref, theirs_ref, *outs):
    places = [(0, index * 512, layer_order[index]) for index in range(5)]
    for copy in cotangent_part(place_ref, cot_ref, places, ([mine_ref], [theirs_ref]), outs):
        copy.wait()


def cotangent_far(
    place_ref, cot_ref, near_ref, near_theirs_ref, far_ref, far_theirs_ref, count_t_ref, *refs
):
    outs = refs[4:]
    places = [(0, 2560, layer_order[5]), (1, 0, layer_order[6]), (1, 512, layer_order[7])]
    parts = ([near_ref, far_ref], [near_theirs_ref, far_theirs_ref])
    copies = cotangent_part(place_ref, cot_ref, places, parts, outs)
    outs[0][...] += nn(count_t_ref[...], outs[1][...]) / 10.0
    for copy in copies:
        copy.wait()


def graph_critical(
    in_ref, count_ref, count_t_ref, one_ref, base_ref, grad_ref, out_ref, cat_ref, own_ref, mean_ref
):
    interleave(in_ref, (nn(count_ref[...], in_ref[...]) / 10.0).astype(bf16), cat_ref)
    pre = nn(cat_ref[...], one_ref[...])
    sigmoid = 1.0 / (1.0 + jnp.exp(-pre))
    out_ref[...] = (pre * sigmoid).astype(bf16)
    pre_grad = (base_ref[...] * (sigmoid * (1.0 + pre * (1.0 - sigmoid)))).astype(bf16)
    layer_backward(pre_grad, one_ref, own_ref, mean_ref)
    spread = nn(count_t_ref[...], mean_ref[...]) / 10.0
    grad_ref[...] = (own_ref[...] + spread).astype(bf16)


def graph_output(first_ref, count_ref, two_ref, out_ref, cat_ref):
    interleave(first_ref, (nn(count_ref[...], first_ref[...]) / 10.0).astype(bf16), cat_ref)
    out_ref[...] = nn(cat_ref[...], two_ref[...]).astype(bf16)


def ff_backward(mine_ref, theirs_ref, put_mine_ref, put_theirs_ref, *refs):
    slope_refs, blocks = refs[:2], units(refs[2:-5])
    grad_ref, own_ref, other_ref, both_ref, pre_ref = refs[-5:]
    summed = nn(put_mine_ref[...], mine_ref[...]) + nn(put_theirs_ref[...], theirs_ref[...])
    both_ref[...] = summed.astype(bf16)
    grad_ref[...] = both_ref[0:128, :]
    for pair in range(8):
        late = pair >= early_blocks // 2
        start = pair * 256 - (early_blocks * 128 if late else 0)
        grown = nt(both_ref[...], out_rows(blocks, pair)) * slope_refs[late][:, start : start + 256]
        pre_ref[:, pair * 256 : pair * 256 + 256] = grown.astype(bf16)
    for column in range(0, 1024, 256):
        at = slice(column, column + 256)
        total = nn(pre_ref[:, 0:256], in_rows(blocks, 0, at))
        for pair in range(1, 8):
            total += nn(pre_ref[:, pair * 256 : pair * 256 + 256], in_rows(blocks, pair, at))
        own_ref[:, at] = total[0:128, :]
        other_ref[:, at] = total[128:256, :]


def finish(states_ref, gain_ref, grad_ref, mine_ref, theirs_ref, out_ref):
    wide = states_ref[...].astype(f32)
    inv_rms = lax.rsqrt(jnp.mean(wide * wide, axis=-1, keepdims=True) + eps_norm)
    scaled = (mine_ref[...] + theirs_ref[...]) * gain_ref[...]
    cubed = inv_rms * inv_rms * inv_rms
    result = (
        grad_ref[...].astype(f32)
        + inv_rms * scaled
        - wide * cubed * jnp.mean(scaled * wide, axis=-1, keepdims=True)
    )
    out_ref[...] = result.astype(bf16)


def on_device(
    node_states,
    norm_gain,
    w_in,
    w_out,
    self_one,
    neigh_one,
    self_two,
    neigh_two,
    send_slots,
    send_counts,
    neighbors,
    out_cotangent,
):
    gain = norm_gain.reshape(1, 1024)
    block, layer_half, place = local_call(
        prepare,
        [shape_of((256, 1024), bf16), shape_of((512, 512), bf16), shape_of((2,), jnp.int32)],
        "hhhhhh",
        "vvs",
        [pltpu.SemaphoreType.DMA((6,))],
        moved=2 << 20,
        limit=60,
    )(w_in, w_out, self_one, neigh_one, self_two, neigh_two)
    filled = jnp.arange(4, dtype=jnp.int32)[None, :] < send_counts[0][:, None]
    own_ids = jnp.where(filled, send_slots, -1).T
    (packed,) = local_call(pack, [shape_of((144, 1024), bf16)], "vv", "v", moved=1 << 20)(
        node_states, own_ids
    )
    blocks, near_parts, far_parts, other_states = gather_weights(block, layer_half, packed)
    pick_mine, put_mine, put_theirs, count, count_t = local_call(
        index_tables,
        [shape_of((128, 256), bf16)] + [shape_of((256, 128), bf16)] * 2 + [shape_of((128, 128), bf16)] * 2,
        "svvv",
        "vvvvv",
        moved=1 << 20,
    )(place, own_ids, other_states, neighbors.T)

    layer_flops = 2 * 128 * 1024 * 2048
    layer_shapes = [
        shape_of((128, 1024), f32),
        shape_of((128, 1024), bf16),
        shape_of((2048, 1024), bf16),
        shape_of((2048, 1024), bf16),
    ]
    layer_sems = [pltpu.SemaphoreType.DMA((10,))] * 2
    near = local_call(
        cotangent_near, layer_shapes, "svvv", "vvvv", layer_sems, flops=layer_flops // 2, moved=10 << 20
    )(place, out_cotangent, *near_parts)

    late_blocks = 16 - early_blocks
    block_flops = 2 * 2 * 256 * 1024 * 128
    early, slope_early, normed = local_call(
        ff_early,
        [
            shape_of((256, 1024), f32),
            shape_of((256, early_blocks * 128), f32),
            shape_of((256, 1024), bf16),
        ],
        "vvv" + "v" * (early_arrays + 1),
        "vvv",
        [pltpu.VMEM((256, early_blocks * 128), bf16)],
        flops=block_flops * early_blocks,
        moved=9 << 20,
    )(node_states, other_states, gain, *blocks[:early_arrays], count_t)
    partial, slope_late = local_call(
        ff_late,
        [shape_of((256, 1024), f32), shape_of((256, late_blocks * 128), f32)],
        "vv" + "v" * (len(blocks) - early_arrays),
        "vv",
        [pltpu.VMEM((256, late_blocks * 128), bf16)],
        flops=block_flops * late_blocks,
        moved=6 << 20,
    )(normed, early, *blocks[early_arrays:])
    partial_theirs = swap(partial)
    base, _, layer_one, layer_two = local_call(
        cotangent_far,
        layer_shapes,
        "svvvvvvvvvv",
        "vvvv",
        layer_sems,
        flops=layer_flops // 2,
        moved=6 << 20,
        aliases={7: 0, 8: 1, 9: 2, 10: 3},
    )(place, out_cotangent, *near_parts, *far_parts, count_t, *near)
    (outgoing,) = local_call(
        pick_rows,
        [shape_of((128, 1024), bf16)],
        "vvvvvv",
        "v",
        flops=2 * 128 * 256 * 1024,
        moved=3 << 20,
    )(node_states, other_states, partial, partial_theirs, pick_mine, base)
    incoming = lax.all_to_all(
        outgoing.reshape(16, 8, 1024), ("x", "y"), split_axis=0, concat_axis=0, tiled=True
    ).reshape(128, 1024)
    slot_grad, first_out = local_call(
        graph_critical,
        [shape_of((128, 1024), bf16), shape_of((128, 1024), bf16)],
        "vvvvv",
        "vv",
        [
            pltpu.VMEM((128, 2048), bf16),
            pltpu.VMEM((128, 1024), f32),
            pltpu.VMEM((128, 1024), bf16),
        ],
        flops=2 * layer_flops,
        moved=5 << 20,
    )(incoming, count, count_t, layer_one, base)
    returned = lax.all_to_all(
        slot_grad.reshape(16, 8, 1024), ("x", "y"), split_axis=0, concat_axis=0, tiled=True
    ).reshape(128, 1024)
    returned_theirs = swap(returned)
    embedded_grad, grad_mine, grad_other = local_call(
        ff_backward,
        [shape_of((128, 1024), bf16), shape_of((128, 1024), f32), shape_of((128, 1024), f32)],
        "vvvvvv" + "v" * len(blocks),
        "vvv",
        [pltpu.VMEM((256, 1024), bf16), pltpu.VMEM((256, 2048), bf16)],
        flops=block_flops * 16,
        moved=14 << 20,
    )(returned, returned_theirs, put_mine, put_theirs, slope_early, slope_late, *blocks)
    grad_theirs = swap(grad_other)
    (node_out,) = local_call(
        graph_output,
        [shape_of((128, 1024), bf16)],
        "vvv",
        "b",
        [pltpu.VMEM((128, 2048), bf16)],
        flops=layer_flops,
        moved=5 << 20,
    )(first_out, count, layer_two)
    (state_grad,) = local_call(
        finish, [shape_of((128, 1024), bf16)], "vvvvv", "b", moved=2 << 20
    )(node_states, gain, embedded_grad, grad_mine, grad_theirs)
    return node_out, state_grad


def solution(mesh):
    split = Mesh(mesh.devices.reshape(4, 4, 2, 8), ("x", "y", "core", "gnn"))
    lm, everywhere = ("x", "y", "core"), ("x", "y", "core", "gnn")
    rows, by_lm, by_gnn = P(everywhere, None), P(lm, None), P("gnn", None)
    return jax.shard_map(
        on_device,
        mesh=split,
        in_specs=(rows, P(), by_lm, by_lm, by_gnn, by_gnn, by_gnn, by_gnn, rows, rows, rows, rows),
        out_specs=(rows, rows),
        check_vma=False,
    )
```

```python
import jax
import jax.numpy as jnp
from jax import lax
from jax.experimental import pallas as pl
from jax.experimental.pallas import tpu as pltpu
from jax.sharding import Mesh
from jax.sharding import PartitionSpec as P

eps_norm = 1e-06
root_coef = 0.7978845608028654
cubic_coef = 0.044715
f32 = jnp.float32
bf16 = jnp.bfloat16

layer_order = (0, -1, 1, -2, 2, -3, 3, -4)
early_arrays = 3
early_blocks = 12


def nt(left, right):
    return lax.dot_general(left, right, (((1,), (1,)), ((), ())), preferred_element_type=f32)


def nn(left, right):
    return jnp.dot(left, right, preferred_element_type=f32)


def local_call(kernel, out_shape, ins, outs, scratch=(), flops=0, moved=0, limit=10, aliases=None):
    specs = {
        "v": pl.BlockSpec(memory_space=pltpu.VMEM),
        "s": pl.BlockSpec(memory_space=pltpu.SMEM),
        "b": pl.BlockSpec(),
        "h": pl.BlockSpec(memory_space=pltpu.HBM),
    }
    return pl.pallas_call(
        kernel,
        out_shape=out_shape,
        in_specs=[specs[kind] for kind in ins],
        out_specs=[specs[kind] for kind in outs],
        scratch_shapes=list(scratch),
        input_output_aliases=aliases or {},
        compiler_params=pltpu.CompilerParams(vmem_limit_bytes=limit * 1024 * 1024),
        cost_estimate=pl.CostEstimate(flops=flops, bytes_accessed=moved, transcendentals=0),
    )


def shape_of(dims, dtype):
    return jax.ShapeDtypeStruct(dims, dtype)


def swap(values):
    return lax.ppermute(values, "core", [(0, 1), (1, 0)])


def shift_plane(values, phase, step):
    pairs = []
    for x in range(4):
        for y in range(4):
            for c in range(2):
                along_x = (phase == 1) == (c == 0)
                to = ((x + step) % 4, y) if along_x else (x, (y + step) % 4)
                pairs.append(((x * 4 + y) * 2 + c, (to[0] * 4 + to[1]) * 2 + c))
    return lax.ppermute(values, ("x", "y", "core"), pairs)


def shift_first(values, step):
    return shift_plane(values, 1, step)


def shift_second(values, step):
    return shift_plane(values, 2, step)


def after(values, *others):
    return lax.optimization_barrier((values, others))[0]


def gather_weights(block, part, states):
    right_1, left_1 = shift_ring(part, 1), shift_ring(part, -1)
    ahead, behind, opposite = shift_first(block, 1), shift_first(block, -1), shift_first(block, 2)
    other_states = swap(states)
    line = join_parts([block, ahead, behind, opposite])

    first = (right_1, left_1, ahead, behind, opposite, other_states)
    right_2 = shift_ring(after(right_1, first), 1)
    left_2 = shift_ring(after(left_1, first), -1)
    right_3 = shift_ring(after(right_1, first), 2)
    line = after(line, first)
    up, down = shift_second(line, 1), shift_second(line, -1)

    second = (right_2, left_2, right_3, up, down)
    left_3 = shift_ring(after(left_2, second), -1)
    right_4 = shift_ring(after(right_3, second), 1)
    far_up = shift_second(after(cut_rows(up, 0), second), 1)
    far_down = shift_second(after(cut_rows(down, 512), second), -1)
    near = join_parts(after([part, right_1, left_1, right_2, left_2, right_3], second))
    near_theirs = swap(near)

    far = [left_3, right_4, far_up, far_down]
    return [line, up, down, far_up, far_down], (near, near_theirs), far, other_states


def shift_ring(values, step):
    pairs = [
        (c * 8 + g, c * 8 + (g + (step if c == 0 else -step)) % 8) for c in range(2) for g in range(8)
    ]
    return lax.ppermute(values, ("core", "gnn"), pairs)


def start_copy(source, target, sem):
    copy = pltpu.make_async_copy(source, target, sem)
    copy.start()
    return copy


def prepare(in_ref, out_ref, *refs):
    block_ref, half_ref, place_ref, sems = refs[4:]
    core = lax.axis_index("core")
    columns = pl.ds(pl.multiple_of(core * 512, 512), 512)
    copies = [
        start_copy(in_ref, block_ref.at[0:128, :], sems.at[0]),
        start_copy(out_ref, block_ref.at[128:256, :], sems.at[1]),
    ]
    for index in range(4):
        target = half_ref.at[index * 128 : index * 128 + 128, :]
        copies.append(start_copy(refs[index].at[:, columns], target, sems.at[2 + index]))
    place_ref[0] = core
    place_ref[1] = lax.axis_index("gnn")
    for copy in copies:
        copy.wait()


def join(*refs):
    rows = refs[0].shape[0]
    for index, ref in enumerate(refs[:-1]):
        refs[-1][index * rows : index * rows + rows, :] = ref[...]


def pack(states_ref, ids_ref, out_ref):
    out_ref[0:128, :] = states_ref[...]
    out_ref[128:144, :] = jnp.zeros((16, 1024), bf16)
    ids = ids_ref[...].astype(f32).astype(bf16)
    rows = (lax.broadcasted_iota(jnp.int32, (16, 4), 0) == lax.broadcasted_iota(jnp.int32, (16, 4), 1)).astype(bf16)
    columns = (lax.broadcasted_iota(jnp.int32, (32, 128), 0) == lax.broadcasted_iota(jnp.int32, (32, 128), 1)).astype(bf16)
    out_ref[128:144, 0:128] = nn(nn(rows, ids).astype(bf16), columns).astype(bf16)


def join_parts(parts):
    rows, columns = parts[0].shape
    (whole,) = local_call(
        join,
        [shape_of((len(parts) * rows, columns), bf16)],
        "v" * len(parts),
        "v",
        moved=len(parts) << 20,
    )(*parts)
    return whole


def cut_rows(values, start):
    def cut(ref, out_ref):
        out_ref[...] = ref[start : start + 512, :]

    (rows,) = local_call(cut, [shape_of((512, 1024), bf16)], "v", "v", moved=2 << 20)(values)
    return rows


def transposed(left, eye):
    return lax.dot_general(left, eye, (((0,), (0,)), ((), ())), preferred_element_type=f32)


def index_tables(place_ref, own_ref, other_ref, neighbors_ref, *refs):
    pick_mine_ref, put_mine_ref, put_theirs_ref, count_ref, count_t_ref = refs
    core = place_ref[0]

    def iota(rows, columns, axis):
        return lax.broadcasted_iota(jnp.int32, (rows, columns), axis)

    eye = (iota(128, 128, 0) == iota(128, 128, 1)).astype(bf16)
    own, other = own_ref[...].astype(f32).astype(bf16), other_ref[128:144, 0:128][0:4, 0:32]
    slot = iota(128, 4, 0) & 3 == iota(128, 4, 1)
    side = (iota(128, 1, 0) >> 2) & 1

    def pick(worker):
        rows = (iota(128, 32, 1) == (iota(128, 32, 0) >> 3) * 2 + worker).astype(bf16)
        own_id = jnp.sum(jnp.where(slot, nt(rows, own), 0.0), axis=1, keepdims=True)
        other_id = jnp.sum(jnp.where(slot, nt(rows, other), 0.0), axis=1, keepdims=True)
        other_id = jnp.where(other_id < 0.0, -1.0, other_id + 128.0)
        ids = jnp.where(side == core, own_id, other_id).astype(jnp.int32)
        return (ids == iota(128, 256, 1)).astype(bf16)

    mine = pick(core)
    pick_mine_ref[...] = mine
    put_mine_ref[...] = transposed(mine, eye).astype(bf16)
    put_theirs_ref[...] = transposed(pick(1 - core), eye).astype(bf16)
    count_t = jnp.zeros((128, 128), f32)
    for index in range(neighbors_ref.shape[0]):
        count_t += (neighbors_ref[index : index + 1, :] == iota(128, 128, 0)).astype(f32)
    count_t = count_t.astype(bf16)
    count_t_ref[...] = count_t
    count_ref[...] = transposed(count_t, eye).astype(bf16)


def units(refs):
    return [(ref, start) for ref in refs for start in range(0, ref.shape[0], 256)]


def in_rows(blocks, pair, at=slice(None)):
    return jnp.concatenate([ref[s : s + 128, at] for ref, s in blocks[2 * pair : 2 * pair + 2]], axis=0)


def out_rows(blocks, pair, at=slice(None)):
    return jnp.concatenate([ref[s + 128 : s + 256, at] for ref, s in blocks[2 * pair : 2 * pair + 2]], axis=0)


def expand_blocks(normed_ref, blocks, slope_ref, act_ref):
    for pair in range(len(blocks) // 2):
        pre = nt(normed_ref[...], in_rows(blocks, pair))
        square = pre * pre
        tangent = jnp.tanh(root_coef * (pre + cubic_coef * square * pre))
        at = slice(pair * 256, pair * 256 + 256)
        act_ref[:, at] = (0.5 * pre * (1.0 + tangent)).astype(bf16)
        slope_ref[:, at] = 0.5 * (1.0 + tangent) + 0.5 * pre * (
            1.0 - tangent * tangent
        ) * root_coef * (1.0 + 3.0 * cubic_coef * square)


def contract_blocks(act_ref, blocks, at):
    total = nn(act_ref[:, 0:256], out_rows(blocks, 0, at))
    for pair in range(1, len(blocks) // 2):
        total += nn(act_ref[:, pair * 256 : pair * 256 + 256], out_rows(blocks, pair, at))
    return total


def ff_early(own_ref, other_ref, gain_ref, *refs):
    blocks = units(refs[:early_arrays])
    partial_ref, slope_ref, normed_ref, act_ref = refs[-4:]
    for part, ref in enumerate((own_ref, other_ref)):
        wide = ref[0:128, :].astype(f32)
        inv_rms = lax.rsqrt(jnp.mean(wide * wide, axis=-1, keepdims=True) + eps_norm)
        normed_ref[part * 128 : part * 128 + 128, :] = (wide * inv_rms * gain_ref[...]).astype(bf16)
    expand_blocks(normed_ref, blocks, slope_ref, act_ref)
    for column in range(0, 1024, 256):
        at = slice(column, column + 256)
        partial_ref[:, at] = contract_blocks(act_ref, blocks, at)


def ff_late(normed_ref, early_ref, *refs):
    partial_ref, slope_ref, act_ref = refs[-3:]
    blocks = units(refs[:-3])
    expand_blocks(normed_ref, blocks, slope_ref, act_ref)
    for column in range(0, 1024, 256):
        at = slice(column, column + 256)
        partial_ref[:, at] = early_ref[:, at] + contract_blocks(act_ref, blocks, at)


def pick_rows(own_ref, other_ref, mine_ref, theirs_ref, pick_ref, _, out_ref):
    own = (own_ref[...].astype(f32) + (mine_ref[0:128, :] + theirs_ref[128:256, :])).astype(bf16)
    other = (other_ref[0:128, :].astype(f32) + (mine_ref[128:256, :] + theirs_ref[0:128, :])).astype(bf16)
    picked = nn(pick_ref[:, 0:128], own) + nn(pick_ref[:, 128:256], other)
    out_ref[...] = picked.astype(bf16)


def interleave(rows_ref, mean, cat_ref):
    for g in range(8):
        at = slice(g * 128, g * 128 + 128)
        cat_ref[:, g * 256 : g * 256 + 128] = rows_ref[:, at]
        cat_ref[:, g * 256 + 128 : g * 256 + 256] = mean[:, at]


def layer_backward(grad, layer_ref, own_ref, mean_ref):
    for g in range(8):
        at = slice(g * 128, g * 128 + 128)
        both = nt(grad, layer_ref[g * 256 : g * 256 + 256, :])
        own_ref[:, at] = both[:, 0:128]
        mean_ref[:, at] = both[:, 128:256].astype(bf16)


def shard_rows(place_ref, offset):
    return pl.multiple_of(lax.rem(place_ref[1] + offset + 8, 8) * 256, 256)


def lay_layer(place_ref, layer, places, refs, layer_ref, sems):
    copies = []
    for half in range(2):
        side = place_ref[0] if half == 0 else 1 - place_ref[0]
        column = pl.multiple_of(side * 512, 512)
        for index, (array, start, offset) in enumerate(places):
            rows = pl.ds(shard_rows(place_ref, (1 - 2 * side) * offset), 256)
            start += layer * 256
            target = layer_ref.at[rows, pl.ds(column, 512)]
            source = refs[half][array].at[start : start + 256, :]
            copies.append(start_copy(source, target, sems.at[half * 5 + index]))
    return copies


def cotangent_part(place_ref, cot_ref, places, refs, outs):
    own_ref, mean_ref, one_ref, two_ref, one_sems, two_sems = outs
    two_copies = lay_layer(place_ref, 1, places, refs, two_ref, two_sems)
    one_copies = lay_layer(place_ref, 0, places, refs, one_ref, one_sems)
    for copy in two_copies:
        copy.wait()
    for _, _, offset in places:
        rows = shard_rows(place_ref, offset)
        at = pl.ds(pl.multiple_of(lax.rem(place_ref[1] + offset + 8, 8) * 128, 128), 128)
        both = nt(cot_ref[...], two_ref[pl.ds(rows, 256), :])
        own_ref[:, at] = both[:, 0:128]
        mean_ref[:, at] = both[:, 128:256].astype(bf16)
    return one_copies


def cotangent_near(place_ref, cot_ref, mine_ref, theirs_ref, *outs):
    places = [(0, index * 512, layer_order[index]) for index in range(5)]
    for copy in cotangent_part(place_ref, cot_ref, places, ([mine_ref], [theirs_ref]), outs):
        copy.wait()


def cotangent_far(
    place_ref, cot_ref, near_ref, near_theirs_ref, far_ref, far_theirs_ref, count_t_ref, *refs
):
    outs = refs[4:]
    places = [(0, 2560, layer_order[5]), (1, 0, layer_order[6]), (1, 512, layer_order[7])]
    parts = ([near_ref, far_ref], [near_theirs_ref, far_theirs_ref])
    copies = cotangent_part(place_ref, cot_ref, places, parts, outs)
    outs[0][...] += nn(count_t_ref[...], outs[1][...]) / 10.0
    for copy in copies:
        copy.wait()


def graph_critical(
    in_ref, count_ref, count_t_ref, one_ref, base_ref, grad_ref, out_ref, cat_ref, own_ref, mean_ref
):
    interleave(in_ref, (nn(count_ref[...], in_ref[...]) / 10.0).astype(bf16), cat_ref)
    pre = nn(cat_ref[...], one_ref[...])
    sigmoid = 1.0 / (1.0 + jnp.exp(-pre))
    out_ref[...] = (pre * sigmoid).astype(bf16)
    pre_grad = (base_ref[...] * (sigmoid * (1.0 + pre * (1.0 - sigmoid)))).astype(bf16)
    layer_backward(pre_grad, one_ref, own_ref, mean_ref)
    spread = nn(count_t_ref[...], mean_ref[...]) / 10.0
    grad_ref[...] = (own_ref[...] + spread).astype(bf16)


def graph_output(first_ref, count_ref, two_ref, out_ref, cat_ref):
    interleave(first_ref, (nn(count_ref[...], first_ref[...]) / 10.0).astype(bf16), cat_ref)
    out_ref[...] = nn(cat_ref[...], two_ref[...]).astype(bf16)


def ff_backward(mine_ref, theirs_ref, put_mine_ref, put_theirs_ref, *refs):
    slope_refs, blocks = refs[:2], units(refs[2:-5])
    grad_ref, own_ref, other_ref, both_ref, pre_ref = refs[-5:]
    summed = nn(put_mine_ref[...], mine_ref[...]) + nn(put_theirs_ref[...], theirs_ref[...])
    both_ref[...] = summed.astype(bf16)
    grad_ref[...] = both_ref[0:128, :]
    for pair in range(8):
        late = pair >= early_blocks // 2
        start = pair * 256 - (early_blocks * 128 if late else 0)
        grown = nt(both_ref[...], out_rows(blocks, pair)) * slope_refs[late][:, start : start + 256]
        pre_ref[:, pair * 256 : pair * 256 + 256] = grown.astype(bf16)
    for column in range(0, 1024, 256):
        at = slice(column, column + 256)
        total = nn(pre_ref[:, 0:256], in_rows(blocks, 0, at))
        for pair in range(1, 8):
            total += nn(pre_ref[:, pair * 256 : pair * 256 + 256], in_rows(blocks, pair, at))
        own_ref[:, at] = total[0:128, :]
        other_ref[:, at] = total[128:256, :]


def finish(states_ref, gain_ref, grad_ref, mine_ref, theirs_ref, out_ref):
    wide = states_ref[...].astype(f32)
    inv_rms = lax.rsqrt(jnp.mean(wide * wide, axis=-1, keepdims=True) + eps_norm)
    scaled = (mine_ref[...] + theirs_ref[...]) * gain_ref[...]
    cubed = inv_rms * inv_rms * inv_rms
    result = (
        grad_ref[...].astype(f32)
        + inv_rms * scaled
        - wide * cubed * jnp.mean(scaled * wide, axis=-1, keepdims=True)
    )
    out_ref[...] = result.astype(bf16)


def on_device(
    node_states,
    norm_gain,
    w_in,
    w_out,
    self_one,
    neigh_one,
    self_two,
    neigh_two,
    send_slots,
    send_counts,
    neighbors,
    out_cotangent,
):
    gain = norm_gain.reshape(1, 1024)
    block, layer_half, place = local_call(
        prepare,
        [shape_of((256, 1024), bf16), shape_of((512, 512), bf16), shape_of((2,), jnp.int32)],
        "hhhhhh",
        "vvs",
        [pltpu.SemaphoreType.DMA((6,))],
        moved=2 << 20,
        limit=60,
    )(w_in, w_out, self_one, neigh_one, self_two, neigh_two)
    filled = jnp.arange(4, dtype=jnp.int32)[None, :] < send_counts[0][:, None]
    own_ids = jnp.where(filled, send_slots, -1).T
    (packed,) = local_call(pack, [shape_of((144, 1024), bf16)], "vv", "v", moved=1 << 20)(
        node_states, own_ids
    )
    blocks, near_parts, far_parts, other_states = gather_weights(block, layer_half, packed)
    pick_mine, put_mine, put_theirs, count, count_t = local_call(
        index_tables,
        [shape_of((128, 256), bf16)] + [shape_of((256, 128), bf16)] * 2 + [shape_of((128, 128), bf16)] * 2,
        "svvv",
        "vvvvv",
        moved=1 << 20,
    )(place, own_ids, other_states, neighbors.T)

    layer_flops = 2 * 128 * 1024 * 2048
    layer_shapes = [
        shape_of((128, 1024), f32),
        shape_of((128, 1024), bf16),
        shape_of((2048, 1024), bf16),
        shape_of((2048, 1024), bf16),
    ]
    layer_sems = [pltpu.SemaphoreType.DMA((10,))] * 2
    near = local_call(
        cotangent_near, layer_shapes, "svvv", "vvvv", layer_sems, flops=layer_flops // 2, moved=10 << 20
    )(place, out_cotangent, *near_parts)

    far = join_parts(after(far_parts[:2], far_parts, near[1]))
    far_parts = (far, swap(far))

    late_blocks = 16 - early_blocks
    block_flops = 2 * 2 * 256 * 1024 * 128
    early, slope_early, normed = local_call(
        ff_early,
        [
            shape_of((256, 1024), f32),
            shape_of((256, early_blocks * 128), f32),
            shape_of((256, 1024), bf16),
        ],
        "vvv" + "v" * (early_arrays + 1),
        "vvv",
        [pltpu.VMEM((256, early_blocks * 128), bf16)],
        flops=block_flops * early_blocks,
        moved=9 << 20,
    )(node_states, other_states, gain, *blocks[:early_arrays], count_t)
    partial, slope_late = local_call(
        ff_late,
        [shape_of((256, 1024), f32), shape_of((256, late_blocks * 128), f32)],
        "vv" + "v" * (len(blocks) - early_arrays),
        "vv",
        [pltpu.VMEM((256, late_blocks * 128), bf16)],
        flops=block_flops * late_blocks,
        moved=6 << 20,
    )(normed, early, *blocks[early_arrays:])
    partial_theirs = swap(partial)
    base, _, layer_one, layer_two = local_call(
        cotangent_far,
        layer_shapes,
        "svvvvvvvvvv",
        "vvvv",
        layer_sems,
        flops=layer_flops // 2,
        moved=6 << 20,
        aliases={7: 0, 8: 1, 9: 2, 10: 3},
    )(place, out_cotangent, *near_parts, *far_parts, count_t, *near)
    (outgoing,) = local_call(
        pick_rows,
        [shape_of((128, 1024), bf16)],
        "vvvvvv",
        "v",
        flops=2 * 128 * 256 * 1024,
        moved=3 << 20,
    )(node_states, other_states, partial, partial_theirs, pick_mine, base)
    incoming = lax.all_to_all(
        outgoing.reshape(16, 8, 1024), ("x", "y"), split_axis=0, concat_axis=0, tiled=True
    ).reshape(128, 1024)
    slot_grad, first_out = local_call(
        graph_critical,
        [shape_of((128, 1024), bf16), shape_of((128, 1024), bf16)],
        "vvvvv",
        "vv",
        [
            pltpu.VMEM((128, 2048), bf16),
            pltpu.VMEM((128, 1024), f32),
            pltpu.VMEM((128, 1024), bf16),
        ],
        flops=2 * layer_flops,
        moved=5 << 20,
    )(incoming, count, count_t, layer_one, base)
    returned = lax.all_to_all(
        slot_grad.reshape(16, 8, 1024), ("x", "y"), split_axis=0, concat_axis=0, tiled=True
    ).reshape(128, 1024)
    returned_theirs = swap(returned)
    embedded_grad, grad_mine, grad_other = local_call(
        ff_backward,
        [shape_of((128, 1024), bf16), shape_of((128, 1024), f32), shape_of((128, 1024), f32)],
        "vvvvvv" + "v" * len(blocks),
        "vvv",
        [pltpu.VMEM((256, 1024), bf16), pltpu.VMEM((256, 2048), bf16)],
        flops=block_flops * 16,
        moved=14 << 20,
    )(returned, returned_theirs, put_mine, put_theirs, slope_early, slope_late, *blocks)
    grad_theirs = swap(grad_other)
    (node_out,) = local_call(
        graph_output,
        [shape_of((128, 1024), bf16)],
        "vvv",
        "b",
        [pltpu.VMEM((128, 2048), bf16)],
        flops=layer_flops,
        moved=5 << 20,
    )(first_out, count, layer_two)
    (state_grad,) = local_call(
        finish, [shape_of((128, 1024), bf16)], "vvvvv", "b", moved=2 << 20
    )(node_states, gain, embedded_grad, grad_mine, grad_theirs)
    return node_out, state_grad


def solution(mesh):
    split = Mesh(mesh.devices.reshape(4, 4, 2, 8), ("x", "y", "core", "gnn"))
    lm, everywhere = ("x", "y", "core"), ("x", "y", "core", "gnn")
    rows, by_lm, by_gnn = P(everywhere, None), P(lm, None), P("gnn", None)
    return jax.shard_map(
        on_device,
        mesh=split,
        in_specs=(rows, P(), by_lm, by_lm, by_gnn, by_gnn, by_gnn, by_gnn, rows, rows, rows, rows),
        out_specs=(rows, rows),
        check_vma=False,
    )
```

```python
import jax
import jax.numpy as jnp
from jax import lax
from jax.experimental import pallas as pl
from jax.experimental.pallas import tpu as pltpu
from jax.sharding import Mesh
from jax.sharding import PartitionSpec as P

eps_norm = 1e-06
root_coef = 0.7978845608028654
cubic_coef = 0.044715
f32 = jnp.float32
bf16 = jnp.bfloat16

layer_order = (0, -1, 1, -2, 2, -3, 3, -4)
early_arrays = 3
early_blocks = 12


def nt(left, right):
    return lax.dot_general(left, right, (((1,), (1,)), ((), ())), preferred_element_type=f32)


def nn(left, right):
    return jnp.dot(left, right, preferred_element_type=f32)


def local_call(kernel, out_shape, ins, outs, scratch=(), flops=0, moved=0, limit=10, aliases=None):
    specs = {
        "v": pl.BlockSpec(memory_space=pltpu.VMEM),
        "s": pl.BlockSpec(memory_space=pltpu.SMEM),
        "b": pl.BlockSpec(),
        "h": pl.BlockSpec(memory_space=pltpu.HBM),
    }
    return pl.pallas_call(
        kernel,
        out_shape=out_shape,
        in_specs=[specs[kind] for kind in ins],
        out_specs=[specs[kind] for kind in outs],
        scratch_shapes=list(scratch),
        input_output_aliases=aliases or {},
        compiler_params=pltpu.CompilerParams(vmem_limit_bytes=limit * 1024 * 1024),
        cost_estimate=pl.CostEstimate(flops=flops, bytes_accessed=moved, transcendentals=0),
    )


def shape_of(dims, dtype):
    return jax.ShapeDtypeStruct(dims, dtype)


def swap(values):
    return lax.ppermute(values, "core", [(0, 1), (1, 0)])


def shift_plane(values, phase, step):
    pairs = []
    for x in range(4):
        for y in range(4):
            for c in range(2):
                along_x = (phase == 1) == (c == 0)
                to = ((x + step) % 4, y) if along_x else (x, (y + step) % 4)
                pairs.append(((x * 4 + y) * 2 + c, (to[0] * 4 + to[1]) * 2 + c))
    return lax.ppermute(values, ("x", "y", "core"), pairs)


def shift_first(values, step):
    return shift_plane(values, 1, step)


def shift_second(values, step):
    return shift_plane(values, 2, step)


def after(values, *others):
    return lax.optimization_barrier((values, others))[0]


def gather_weights(block, part, states):
    right_1, left_1 = shift_ring(part, 1), shift_ring(part, -1)
    ahead, behind, opposite = shift_first(block, 1), shift_first(block, -1), shift_first(block, 2)
    other_states = swap(states)
    line = fill_line(open_line(block), ahead, behind, opposite)

    first = (right_1, left_1, ahead, behind, opposite, other_states)
    right_2 = shift_ring(after(right_1, first), 1)
    left_2 = shift_ring(after(left_1, first), -1)
    right_3 = shift_ring(after(right_1, first), 2)
    line = after(line, first)
    up, down = shift_second(line, 1), shift_second(line, -1)

    second = (right_2, left_2, right_3, up, down)
    left_3 = shift_ring(after(left_2, second), -1)
    right_4 = shift_ring(after(right_3, second), 1)
    far_up = shift_second(after(cut_rows(up, 0), second), 1)
    far_down = shift_second(after(cut_rows(down, 512), second), -1)
    near = join_parts(after([part, right_1, left_1, right_2, left_2, right_3], second))
    near_theirs = swap(near)

    far = [left_3, right_4, far_up, far_down]
    return [line, up, down, far_up, far_down], (near, near_theirs), far, other_states


def shift_ring(values, step):
    pairs = [
        (c * 8 + g, c * 8 + (g + (step if c == 0 else -step)) % 8) for c in range(2) for g in range(8)
    ]
    return lax.ppermute(values, ("core", "gnn"), pairs)


def start_copy(source, target, sem):
    copy = pltpu.make_async_copy(source, target, sem)
    copy.start()
    return copy


def prepare(in_ref, out_ref, *refs):
    block_ref, half_ref, place_ref, sems = refs[4:]
    core = lax.axis_index("core")
    columns = pl.ds(pl.multiple_of(core * 512, 512), 512)
    copies = [
        start_copy(in_ref, block_ref.at[0:128, :], sems.at[0]),
        start_copy(out_ref, block_ref.at[128:256, :], sems.at[1]),
    ]
    for index in range(4):
        target = half_ref.at[index * 128 : index * 128 + 128, :]
        copies.append(start_copy(refs[index].at[:, columns], target, sems.at[2 + index]))
    place_ref[0] = core
    place_ref[1] = lax.axis_index("gnn")
    for copy in copies:
        copy.wait()


def join(*refs):
    rows = refs[0].shape[0]
    for index, ref in enumerate(refs[:-1]):
        refs[-1][index * rows : index * rows + rows, :] = ref[...]


def pack(states_ref, ids_ref, out_ref):
    out_ref[0:128, :] = states_ref[...]
    out_ref[128:144, :] = jnp.zeros((16, 1024), bf16)
    ids = ids_ref[...].astype(f32).astype(bf16)
    rows = (lax.broadcasted_iota(jnp.int32, (16, 4), 0) == lax.broadcasted_iota(jnp.int32, (16, 4), 1)).astype(bf16)
    columns = (lax.broadcasted_iota(jnp.int32, (32, 128), 0) == lax.broadcasted_iota(jnp.int32, (32, 128), 1)).astype(bf16)
    out_ref[128:144, 0:128] = nn(nn(rows, ids).astype(bf16), columns).astype(bf16)


def join_parts(parts):
    rows, columns = parts[0].shape
    (whole,) = local_call(
        join,
        [shape_of((len(parts) * rows, columns), bf16)],
        "v" * len(parts),
        "v",
        moved=len(parts) << 20,
    )(*parts)
    return whole


def cut_rows(values, start):
    def cut(ref, out_ref):
        out_ref[...] = ref[start : start + 512, :]

    (rows,) = local_call(cut, [shape_of((512, 1024), bf16)], "v", "v", moved=2 << 20)(values)
    return rows


def open_line(block):
    def open_up(ref, out_ref):
        out_ref[0:256, :] = ref[...]

    (line,) = local_call(open_up, [shape_of((1024, 1024), bf16)], "v", "v", moved=1 << 20)(block)
    return line


def fill_line(line, *blocks):
    def fill(_, *refs):
        for index, ref in enumerate(refs[:-1]):
            refs[-1][index * 256 + 256 : index * 256 + 512, :] = ref[...]

    (line,) = local_call(
        fill, [shape_of((1024, 1024), bf16)], "vvvv", "v", moved=3 << 20, aliases={0: 0}
    )(line, *blocks)
    return line


def transposed(left, eye):
    return lax.dot_general(left, eye, (((0,), (0,)), ((), ())), preferred_element_type=f32)


def index_tables(place_ref, own_ref, other_ref, neighbors_ref, *refs):
    pick_mine_ref, put_mine_ref, put_theirs_ref, count_ref, count_t_ref = refs
    core = place_ref[0]

    def iota(rows, columns, axis):
        return lax.broadcasted_iota(jnp.int32, (rows, columns), axis)

    eye = (iota(128, 128, 0) == iota(128, 128, 1)).astype(bf16)
    own, other = own_ref[...].astype(f32).astype(bf16), other_ref[128:144, 0:128][0:4, 0:32]
    slot = iota(128, 4, 0) & 3 == iota(128, 4, 1)
    side = (iota(128, 1, 0) >> 2) & 1

    def pick(worker):
        rows = (iota(128, 32, 1) == (iota(128, 32, 0) >> 3) * 2 + worker).astype(bf16)
        own_id = jnp.sum(jnp.where(slot, nt(rows, own), 0.0), axis=1, keepdims=True)
        other_id = jnp.sum(jnp.where(slot, nt(rows, other), 0.0), axis=1, keepdims=True)
        other_id = jnp.where(other_id < 0.0, -1.0, other_id + 128.0)
        ids = jnp.where(side == core, own_id, other_id).astype(jnp.int32)
        return (ids == iota(128, 256, 1)).astype(bf16)

    mine = pick(core)
    pick_mine_ref[...] = mine
    put_mine_ref[...] = transposed(mine, eye).astype(bf16)
    put_theirs_ref[...] = transposed(pick(1 - core), eye).astype(bf16)
    count_t = jnp.zeros((128, 128), f32)
    for index in range(neighbors_ref.shape[0]):
        count_t += (neighbors_ref[index : index + 1, :] == iota(128, 128, 0)).astype(f32)
    count_t = count_t.astype(bf16)
    count_t_ref[...] = count_t
    count_ref[...] = transposed(count_t, eye).astype(bf16)


def units(refs):
    return [(ref, start) for ref in refs for start in range(0, ref.shape[0], 256)]


def in_rows(blocks, pair, at=slice(None)):
    return jnp.concatenate([ref[s : s + 128, at] for ref, s in blocks[2 * pair : 2 * pair + 2]], axis=0)


def out_rows(blocks, pair, at=slice(None)):
    return jnp.concatenate([ref[s + 128 : s + 256, at] for ref, s in blocks[2 * pair : 2 * pair + 2]], axis=0)


def expand_blocks(normed_ref, blocks, slope_ref, act_ref):
    for pair in range(len(blocks) // 2):
        pre = nt(normed_ref[...], in_rows(blocks, pair))
        square = pre * pre
        tangent = jnp.tanh(root_coef * (pre + cubic_coef * square * pre))
        at = slice(pair * 256, pair * 256 + 256)
        act_ref[:, at] = (0.5 * pre * (1.0 + tangent)).astype(bf16)
        slope_ref[:, at] = 0.5 * (1.0 + tangent) + 0.5 * pre * (
            1.0 - tangent * tangent
        ) * root_coef * (1.0 + 3.0 * cubic_coef * square)


def contract_blocks(act_ref, blocks, at):
    total = nn(act_ref[:, 0:256], out_rows(blocks, 0, at))
    for pair in range(1, len(blocks) // 2):
        total += nn(act_ref[:, pair * 256 : pair * 256 + 256], out_rows(blocks, pair, at))
    return total


def ff_early(own_ref, other_ref, gain_ref, *refs):
    blocks = units(refs[:early_arrays])
    partial_ref, slope_ref, normed_ref, act_ref = refs[-4:]
    for part, ref in enumerate((own_ref, other_ref)):
        wide = ref[0:128, :].astype(f32)
        inv_rms = lax.rsqrt(jnp.mean(wide * wide, axis=-1, keepdims=True) + eps_norm)
        normed_ref[part * 128 : part * 128 + 128, :] = (wide * inv_rms * gain_ref[...]).astype(bf16)
    expand_blocks(normed_ref, blocks, slope_ref, act_ref)
    for column in range(0, 1024, 256):
        at = slice(column, column + 256)
        partial_ref[:, at] = contract_blocks(act_ref, blocks, at)


def ff_late(normed_ref, early_ref, *refs):
    partial_ref, slope_ref, act_ref = refs[-3:]
    blocks = units(refs[:-3])
    expand_blocks(normed_ref, blocks, slope_ref, act_ref)
    for column in range(0, 1024, 256):
        at = slice(column, column + 256)
        partial_ref[:, at] = early_ref[:, at] + contract_blocks(act_ref, blocks, at)


def pick_rows(own_ref, other_ref, mine_ref, theirs_ref, pick_ref, _, out_ref):
    own = (own_ref[...].astype(f32) + (mine_ref[0:128, :] + theirs_ref[128:256, :])).astype(bf16)
    other = (other_ref[0:128, :].astype(f32) + (mine_ref[128:256, :] + theirs_ref[0:128, :])).astype(bf16)
    picked = nn(pick_ref[:, 0:128], own) + nn(pick_ref[:, 128:256], other)
    out_ref[...] = picked.astype(bf16)


def interleave(rows_ref, mean, cat_ref):
    for g in range(8):
        at = slice(g * 128, g * 128 + 128)
        cat_ref[:, g * 256 : g * 256 + 128] = rows_ref[:, at]
        cat_ref[:, g * 256 + 128 : g * 256 + 256] = mean[:, at]


def layer_backward(grad, layer_ref, own_ref, mean_ref):
    for g in range(8):
        at = slice(g * 128, g * 128 + 128)
        both = nt(grad, layer_ref[g * 256 : g * 256 + 256, :])
        own_ref[:, at] = both[:, 0:128]
        mean_ref[:, at] = both[:, 128:256].astype(bf16)


def shard_rows(place_ref, offset):
    return pl.multiple_of(lax.rem(place_ref[1] + offset + 8, 8) * 256, 256)


def lay_layer(place_ref, layer, places, refs, layer_ref, sems):
    copies = []
    for half in range(2):
        side = place_ref[0] if half == 0 else 1 - place_ref[0]
        column = pl.multiple_of(side * 512, 512)
        for index, (array, start, offset) in enumerate(places):
            rows = pl.ds(shard_rows(place_ref, (1 - 2 * side) * offset), 256)
            start += layer * 256
            target = layer_ref.at[rows, pl.ds(column, 512)]
            source = refs[half][array].at[start : start + 256, :]
            copies.append(start_copy(source, target, sems.at[half * 5 + index]))
    return copies


def cotangent_part(place_ref, cot_ref, places, refs, outs):
    own_ref, mean_ref, one_ref, two_ref, one_sems, two_sems = outs
    two_copies = lay_layer(place_ref, 1, places, refs, two_ref, two_sems)
    one_copies = lay_layer(place_ref, 0, places, refs, one_ref, one_sems)
    for copy in two_copies:
        copy.wait()
    for _, _, offset in places:
        rows = shard_rows(place_ref, offset)
        at = pl.ds(pl.multiple_of(lax.rem(place_ref[1] + offset + 8, 8) * 128, 128), 128)
        both = nt(cot_ref[...], two_ref[pl.ds(rows, 256), :])
        own_ref[:, at] = both[:, 0:128]
        mean_ref[:, at] = both[:, 128:256].astype(bf16)
    return one_copies


def cotangent_near(place_ref, cot_ref, mine_ref, theirs_ref, *outs):
    places = [(0, index * 512, layer_order[index]) for index in range(5)]
    for copy in cotangent_part(place_ref, cot_ref, places, ([mine_ref], [theirs_ref]), outs):
        copy.wait()


def cotangent_far(
    place_ref, cot_ref, near_ref, near_theirs_ref, far_ref, far_theirs_ref, count_t_ref, *refs
):
    own_ref, mean_ref, one_ref, two_ref = refs[4:]
    parts = ((near_ref, far_ref), (near_theirs_ref, far_theirs_ref))
    starts = ((0, 2560), (1, 0), (1, 512))
    grads = []
    for half in range(2):
        side = place_ref[0] if half == 0 else 1 - place_ref[0]
        column = pl.ds(pl.multiple_of(side * 512, 512), 512)
        cot = cot_ref[:, column]
        grads.append([])
        for (array, start), offset in zip(starts, layer_order[5:], strict=True):
            rows = pl.ds(shard_rows(place_ref, (1 - 2 * side) * offset), 256)
            one, two = slice(start, start + 256), slice(start + 256, start + 512)
            one_ref[rows, column] = parts[half][array][one, :]
            two_ref[rows, column] = parts[half][array][two, :]
            grads[half].append(nt(cot, parts[half][array][two, :]))
    for index, offset in enumerate(layer_order[5:]):
        both = grads[0][index] + grads[1][(1, 0, 2)[index]]
        shard = lax.rem(place_ref[1] + (1 - 2 * place_ref[0]) * offset + 8, 8)
        at = pl.ds(pl.multiple_of(shard * 128, 128), 128)
        own_ref[:, at] = both[:, 0:128]
        mean_ref[:, at] = both[:, 128:256].astype(bf16)
    own_ref[...] += nn(count_t_ref[...], mean_ref[...]) / 10.0


def graph_critical(
    in_ref, count_ref, count_t_ref, one_ref, base_ref, grad_ref, out_ref, cat_ref, own_ref, mean_ref
):
    interleave(in_ref, (nn(count_ref[...], in_ref[...]) / 10.0).astype(bf16), cat_ref)
    pre = nn(cat_ref[...], one_ref[...])
    sigmoid = 1.0 / (1.0 + jnp.exp(-pre))
    out_ref[...] = (pre * sigmoid).astype(bf16)
    pre_grad = (base_ref[...] * (sigmoid * (1.0 + pre * (1.0 - sigmoid)))).astype(bf16)
    layer_backward(pre_grad, one_ref, own_ref, mean_ref)
    spread = nn(count_t_ref[...], mean_ref[...]) / 10.0
    grad_ref[...] = (own_ref[...] + spread).astype(bf16)


def graph_output(first_ref, count_ref, two_ref, out_ref, cat_ref):
    interleave(first_ref, (nn(count_ref[...], first_ref[...]) / 10.0).astype(bf16), cat_ref)
    out_ref[...] = nn(cat_ref[...], two_ref[...]).astype(bf16)


def ff_backward(mine_ref, theirs_ref, put_mine_ref, put_theirs_ref, *refs):
    slope_refs, blocks = refs[:2], units(refs[2:-5])
    grad_ref, own_ref, other_ref, both_ref, pre_ref = refs[-5:]
    summed = nn(put_mine_ref[...], mine_ref[...]) + nn(put_theirs_ref[...], theirs_ref[...])
    both_ref[...] = summed.astype(bf16)
    grad_ref[...] = both_ref[0:128, :]
    for pair in range(8):
        late = pair >= early_blocks // 2
        start = pair * 256 - (early_blocks * 128 if late else 0)
        grown = nt(both_ref[...], out_rows(blocks, pair)) * slope_refs[late][:, start : start + 256]
        pre_ref[:, pair * 256 : pair * 256 + 256] = grown.astype(bf16)
    for column in range(0, 1024, 256):
        at = slice(column, column + 256)
        total = nn(pre_ref[:, 0:256], in_rows(blocks, 0, at))
        for pair in range(1, 8):
            total += nn(pre_ref[:, pair * 256 : pair * 256 + 256], in_rows(blocks, pair, at))
        own_ref[:, at] = total[0:128, :]
        other_ref[:, at] = total[128:256, :]


def finish(states_ref, gain_ref, grad_ref, mine_ref, theirs_ref, out_ref):
    wide = states_ref[...].astype(f32)
    inv_rms = lax.rsqrt(jnp.mean(wide * wide, axis=-1, keepdims=True) + eps_norm)
    scaled = (mine_ref[...] + theirs_ref[...]) * gain_ref[...]
    cubed = inv_rms * inv_rms * inv_rms
    result = (
        grad_ref[...].astype(f32)
        + inv_rms * scaled
        - wide * cubed * jnp.mean(scaled * wide, axis=-1, keepdims=True)
    )
    out_ref[...] = result.astype(bf16)


def on_device(
    node_states,
    norm_gain,
    w_in,
    w_out,
    self_one,
    neigh_one,
    self_two,
    neigh_two,
    send_slots,
    send_counts,
    neighbors,
    out_cotangent,
):
    gain = norm_gain.reshape(1, 1024)
    block, layer_half, place = local_call(
        prepare,
        [shape_of((256, 1024), bf16), shape_of((512, 512), bf16), shape_of((2,), jnp.int32)],
        "hhhhhh",
        "vvs",
        [pltpu.SemaphoreType.DMA((6,))],
        moved=2 << 20,
        limit=60,
    )(w_in, w_out, self_one, neigh_one, self_two, neigh_two)
    filled = jnp.arange(4, dtype=jnp.int32)[None, :] < send_counts[0][:, None]
    own_ids = jnp.where(filled, send_slots, -1).T
    (packed,) = local_call(pack, [shape_of((144, 1024), bf16)], "vv", "v", moved=1 << 20)(
        node_states, own_ids
    )
    blocks, near_parts, far_parts, other_states = gather_weights(block, layer_half, packed)
    pick_mine, put_mine, put_theirs, count, count_t = local_call(
        index_tables,
        [shape_of((128, 256), bf16)] + [shape_of((256, 128), bf16)] * 2 + [shape_of((128, 128), bf16)] * 2,
        "svvv",
        "vvvvv",
        moved=1 << 20,
    )(place, own_ids, other_states, neighbors.T)

    layer_flops = 2 * 128 * 1024 * 2048
    layer_shapes = [
        shape_of((128, 1024), f32),
        shape_of((128, 1024), bf16),
        shape_of((2048, 1024), bf16),
        shape_of((2048, 1024), bf16),
    ]
    layer_sems = [pltpu.SemaphoreType.DMA((10,))] * 2
    near = local_call(
        cotangent_near, layer_shapes, "svvv", "vvvv", layer_sems, flops=layer_flops // 2, moved=10 << 20
    )(place, out_cotangent, *near_parts)

    far = join_parts(after(far_parts[:2], far_parts, near[1]))
    far_parts = (far, swap(far))

    late_blocks = 16 - early_blocks
    block_flops = 2 * 2 * 256 * 1024 * 128
    early, slope_early, normed = local_call(
        ff_early,
        [
            shape_of((256, 1024), f32),
            shape_of((256, early_blocks * 128), f32),
            shape_of((256, 1024), bf16),
        ],
        "vvv" + "v" * (early_arrays + 1),
        "vvv",
        [pltpu.VMEM((256, early_blocks * 128), bf16)],
        flops=block_flops * early_blocks,
        moved=9 << 20,
    )(node_states, other_states, gain, *blocks[:early_arrays], count_t)
    partial, slope_late = local_call(
        ff_late,
        [shape_of((256, 1024), f32), shape_of((256, late_blocks * 128), f32)],
        "vv" + "v" * (len(blocks) - early_arrays),
        "vv",
        [pltpu.VMEM((256, late_blocks * 128), bf16)],
        flops=block_flops * late_blocks,
        moved=6 << 20,
    )(normed, early, *blocks[early_arrays:])
    partial_theirs = swap(partial)
    base, _, layer_one, layer_two = local_call(
        cotangent_far,
        layer_shapes,
        "svvvvvvvvvv",
        "vvvv",
        [],
        flops=layer_flops // 2,
        moved=6 << 20,
        aliases={7: 0, 8: 1, 9: 2, 10: 3},
    )(place, out_cotangent, *near_parts, *far_parts, count_t, *near)
    (outgoing,) = local_call(
        pick_rows,
        [shape_of((128, 1024), bf16)],
        "vvvvvv",
        "v",
        flops=2 * 128 * 256 * 1024,
        moved=3 << 20,
    )(node_states, other_states, partial, partial_theirs, pick_mine, base)
    incoming = lax.all_to_all(
        outgoing.reshape(16, 8, 1024), ("x", "y"), split_axis=0, concat_axis=0, tiled=True
    ).reshape(128, 1024)
    slot_grad, first_out = local_call(
        graph_critical,
        [shape_of((128, 1024), bf16), shape_of((128, 1024), bf16)],
        "vvvvv",
        "vv",
        [
            pltpu.VMEM((128, 2048), bf16),
            pltpu.VMEM((128, 1024), f32),
            pltpu.VMEM((128, 1024), bf16),
        ],
        flops=2 * layer_flops,
        moved=5 << 20,
    )(incoming, count, count_t, layer_one, base)
    returned = lax.all_to_all(
        slot_grad.reshape(16, 8, 1024), ("x", "y"), split_axis=0, concat_axis=0, tiled=True
    ).reshape(128, 1024)
    returned_theirs = swap(returned)
    embedded_grad, grad_mine, grad_other = local_call(
        ff_backward,
        [shape_of((128, 1024), bf16), shape_of((128, 1024), f32), shape_of((128, 1024), f32)],
        "vvvvvv" + "v" * len(blocks),
        "vvv",
        [pltpu.VMEM((256, 1024), bf16), pltpu.VMEM((256, 2048), bf16)],
        flops=block_flops * 16,
        moved=14 << 20,
    )(returned, returned_theirs, put_mine, put_theirs, slope_early, slope_late, *blocks)
    grad_theirs = swap(grad_other)
    (node_out,) = local_call(
        graph_output,
        [shape_of((128, 1024), bf16)],
        "vvv",
        "b",
        [pltpu.VMEM((128, 2048), bf16)],
        flops=layer_flops,
        moved=5 << 20,
    )(first_out, count, layer_two)
    (state_grad,) = local_call(
        finish, [shape_of((128, 1024), bf16)], "vvvvv", "b", moved=2 << 20
    )(node_states, gain, embedded_grad, grad_mine, grad_theirs)
    return node_out, state_grad


def solution(mesh):
    split = Mesh(mesh.devices.reshape(4, 4, 2, 8), ("x", "y", "core", "gnn"))
    lm, everywhere = ("x", "y", "core"), ("x", "y", "core", "gnn")
    rows, by_lm, by_gnn = P(everywhere, None), P(lm, None), P("gnn", None)
    return jax.shard_map(
        on_device,
        mesh=split,
        in_specs=(rows, P(), by_lm, by_lm, by_gnn, by_gnn, by_gnn, by_gnn, rows, rows, rows, rows),
        out_specs=(rows, rows),
        check_vma=False,
    )
```

```python
import jax
import jax.numpy as jnp
from jax import lax
from jax.experimental import pallas as pl
from jax.experimental.pallas import tpu as pltpu
from jax.sharding import Mesh
from jax.sharding import PartitionSpec as P

eps_norm = 1e-06
root_coef = 0.7978845608028654
cubic_coef = 0.044715
f32 = jnp.float32
bf16 = jnp.bfloat16

layer_order = (0, -1, 1, -2, 2, -3, 3, -4)
early_arrays = 3
early_blocks = 12


def nt(left, right):
    return lax.dot_general(left, right, (((1,), (1,)), ((), ())), preferred_element_type=f32)


def nn(left, right):
    return jnp.dot(left, right, preferred_element_type=f32)


def local_call(kernel, out_shape, ins, outs, scratch=(), flops=0, moved=0, limit=10, aliases=None):
    specs = {
        "v": pl.BlockSpec(memory_space=pltpu.VMEM),
        "s": pl.BlockSpec(memory_space=pltpu.SMEM),
        "b": pl.BlockSpec(),
        "h": pl.BlockSpec(memory_space=pltpu.HBM),
    }
    return pl.pallas_call(
        kernel,
        out_shape=out_shape,
        in_specs=[specs[kind] for kind in ins],
        out_specs=[specs[kind] for kind in outs],
        scratch_shapes=list(scratch),
        input_output_aliases=aliases or {},
        compiler_params=pltpu.CompilerParams(vmem_limit_bytes=limit * 1024 * 1024),
        cost_estimate=pl.CostEstimate(flops=flops, bytes_accessed=moved, transcendentals=0),
    )


def shape_of(dims, dtype):
    return jax.ShapeDtypeStruct(dims, dtype)


def swap(values):
    return lax.ppermute(values, "core", [(0, 1), (1, 0)])


def shift_plane(values, phase, step):
    pairs = []
    for x in range(4):
        for y in range(4):
            for c in range(2):
                along_x = (phase == 1) == (c == 0)
                to = ((x + step) % 4, y) if along_x else (x, (y + step) % 4)
                pairs.append(((x * 4 + y) * 2 + c, (to[0] * 4 + to[1]) * 2 + c))
    return lax.ppermute(values, ("x", "y", "core"), pairs)


def shift_first(values, step):
    return shift_plane(values, 1, step)


def shift_second(values, step):
    return shift_plane(values, 2, step)


def after(values, *others):
    return lax.optimization_barrier((values, others))[0]


def gather_weights(block, part, states):
    right_1, left_1 = shift_ring(part, 1), shift_ring(part, -1)
    ahead, behind, opposite = shift_first(block, 1), shift_first(block, -1), shift_first(block, 2)
    other_states = swap(states)
    line = fill_line(open_line(block), ahead, behind, opposite)

    first = (right_1, left_1, ahead, behind, opposite, other_states)
    right_2 = shift_ring(after(right_1, first), 1)
    left_2 = shift_ring(after(left_1, first), -1)
    right_3 = shift_ring(after(right_1, first), 2)
    line = after(line, first)
    up, down = shift_second(line, 1), shift_second(line, -1)

    second = (right_2, left_2, right_3, up, down)
    left_3 = shift_ring(after(left_2, second), -1)
    right_4 = shift_ring(after(right_3, second), 1)
    far_up = shift_second(after(cut_rows(up, 0), second), 1)
    far_down = shift_second(after(cut_rows(down, 512), second), -1)
    near = join_parts(after([part, right_1, left_1, right_2, left_2, right_3], second))
    near_theirs = swap(near)

    far = [left_3, right_4, far_up, far_down]
    return [line, up, down, far_up, far_down], (near, near_theirs), far, other_states


def shift_ring(values, step):
    pairs = [
        (c * 8 + g, c * 8 + (g + (step if c == 0 else -step)) % 8) for c in range(2) for g in range(8)
    ]
    return lax.ppermute(values, ("core", "gnn"), pairs)


def start_copy(source, target, sem):
    copy = pltpu.make_async_copy(source, target, sem)
    copy.start()
    return copy


def prepare(in_ref, out_ref, *refs):
    block_ref, half_ref, place_ref, sems = refs[4:]
    core = lax.axis_index("core")
    columns = pl.ds(pl.multiple_of(core * 512, 512), 512)
    copies = [
        start_copy(in_ref, block_ref.at[0:128, :], sems.at[0]),
        start_copy(out_ref, block_ref.at[128:256, :], sems.at[1]),
    ]
    for index in range(4):
        target = half_ref.at[index * 128 : index * 128 + 128, :]
        copies.append(start_copy(refs[index].at[:, columns], target, sems.at[2 + index]))
    place_ref[0] = core
    place_ref[1] = lax.axis_index("gnn")
    for copy in copies:
        copy.wait()


def join(*refs):
    rows = refs[0].shape[0]
    for index, ref in enumerate(refs[:-1]):
        refs[-1][index * rows : index * rows + rows, :] = ref[...]


def pack(states_ref, ids_ref, out_ref):
    out_ref[0:128, :] = states_ref[...]
    out_ref[128:144, :] = jnp.zeros((16, 1024), bf16)
    ids = ids_ref[...].astype(f32).astype(bf16)
    rows = (lax.broadcasted_iota(jnp.int32, (16, 4), 0) == lax.broadcasted_iota(jnp.int32, (16, 4), 1)).astype(bf16)
    columns = (lax.broadcasted_iota(jnp.int32, (32, 128), 0) == lax.broadcasted_iota(jnp.int32, (32, 128), 1)).astype(bf16)
    out_ref[128:144, 0:128] = nn(nn(rows, ids).astype(bf16), columns).astype(bf16)


def join_parts(parts):
    rows, columns = parts[0].shape
    (whole,) = local_call(
        join,
        [shape_of((len(parts) * rows, columns), bf16)],
        "v" * len(parts),
        "v",
        moved=len(parts) << 20,
    )(*parts)
    return whole


def cut_rows(values, start):
    def cut(ref, out_ref):
        out_ref[...] = ref[start : start + 512, :]

    (rows,) = local_call(cut, [shape_of((512, 1024), bf16)], "v", "v", moved=2 << 20)(values)
    return rows


def open_line(block):
    def open_up(ref, out_ref):
        out_ref[0:256, :] = ref[...]

    (line,) = local_call(open_up, [shape_of((1024, 1024), bf16)], "v", "v", moved=1 << 20)(block)
    return line


def fill_line(line, *blocks):
    def fill(_, *refs):
        for index, ref in enumerate(refs[:-1]):
            refs[-1][index * 256 + 256 : index * 256 + 512, :] = ref[...]

    (line,) = local_call(
        fill, [shape_of((1024, 1024), bf16)], "vvvv", "v", moved=3 << 20, aliases={0: 0}
    )(line, *blocks)
    return line


def transposed(left, eye):
    return lax.dot_general(left, eye, (((0,), (0,)), ((), ())), preferred_element_type=f32)


def index_tables(place_ref, own_ref, other_ref, neighbors_ref, *refs):
    pick_mine_ref, put_mine_ref, put_theirs_ref, count_ref, count_t_ref = refs
    core = place_ref[0]

    def iota(rows, columns, axis):
        return lax.broadcasted_iota(jnp.int32, (rows, columns), axis)

    eye = (iota(128, 128, 0) == iota(128, 128, 1)).astype(bf16)
    own, other = own_ref[...].astype(f32).astype(bf16), other_ref[128:144, 0:128][0:4, 0:32]
    slot = iota(128, 4, 0) & 3 == iota(128, 4, 1)
    side = (iota(128, 1, 0) >> 2) & 1

    def pick(worker):
        rows = (iota(128, 32, 1) == (iota(128, 32, 0) >> 3) * 2 + worker).astype(bf16)
        own_id = jnp.sum(jnp.where(slot, nt(rows, own), 0.0), axis=1, keepdims=True)
        other_id = jnp.sum(jnp.where(slot, nt(rows, other), 0.0), axis=1, keepdims=True)
        other_id = jnp.where(other_id < 0.0, -1.0, other_id + 128.0)
        ids = jnp.where(side == core, own_id, other_id).astype(jnp.int32)
        return (ids == iota(128, 256, 1)).astype(bf16)

    mine = pick(core)
    pick_mine_ref[...] = mine
    put_mine_ref[...] = transposed(mine, eye).astype(bf16)
    put_theirs_ref[...] = transposed(pick(1 - core), eye).astype(bf16)
    count_t = jnp.zeros((128, 128), f32)
    for index in range(neighbors_ref.shape[0]):
        count_t += (neighbors_ref[index : index + 1, :] == iota(128, 128, 0)).astype(f32)
    count_t = count_t.astype(bf16)
    count_t_ref[...] = count_t
    count_ref[...] = transposed(count_t, eye).astype(bf16)


def units(refs):
    return [(ref, start) for ref in refs for start in range(0, ref.shape[0], 256)]


def in_rows(blocks, pair, at=slice(None)):
    return jnp.concatenate([ref[s : s + 128, at] for ref, s in blocks[2 * pair : 2 * pair + 2]], axis=0)


def out_rows(blocks, pair, at=slice(None)):
    return jnp.concatenate([ref[s + 128 : s + 256, at] for ref, s in blocks[2 * pair : 2 * pair + 2]], axis=0)


def expand_blocks(normed_ref, blocks, slope_ref, act_ref):
    for pair in range(len(blocks) // 2):
        pre = nt(normed_ref[...], in_rows(blocks, pair))
        square = pre * pre
        tangent = jnp.tanh(root_coef * (pre + cubic_coef * square * pre))
        at = slice(pair * 256, pair * 256 + 256)
        act_ref[:, at] = (0.5 * pre * (1.0 + tangent)).astype(bf16)
        slope_ref[:, at] = 0.5 * (1.0 + tangent) + 0.5 * pre * (
            1.0 - tangent * tangent
        ) * root_coef * (1.0 + 3.0 * cubic_coef * square)


def contract_blocks(act_ref, blocks, at):
    total = nn(act_ref[:, 0:256], out_rows(blocks, 0, at))
    for pair in range(1, len(blocks) // 2):
        total += nn(act_ref[:, pair * 256 : pair * 256 + 256], out_rows(blocks, pair, at))
    return total


def ff_early(own_ref, other_ref, gain_ref, *refs):
    blocks = units(refs[:early_arrays])
    partial_ref, slope_ref, normed_ref, act_ref = refs[-4:]
    for part, ref in enumerate((own_ref, other_ref)):
        wide = ref[0:128, :].astype(f32)
        inv_rms = lax.rsqrt(jnp.mean(wide * wide, axis=-1, keepdims=True) + eps_norm)
        normed_ref[part * 128 : part * 128 + 128, :] = (wide * inv_rms * gain_ref[...]).astype(bf16)
    expand_blocks(normed_ref, blocks, slope_ref, act_ref)
    for column in range(0, 1024, 256):
        at = slice(column, column + 256)
        partial_ref[:, at] = contract_blocks(act_ref, blocks, at)


def ff_late(normed_ref, early_ref, *refs):
    partial_ref, slope_ref, act_ref = refs[-3:]
    blocks = units(refs[:-3])
    expand_blocks(normed_ref, blocks, slope_ref, act_ref)
    for column in range(0, 1024, 256):
        at = slice(column, column + 256)
        partial_ref[:, at] = early_ref[:, at] + contract_blocks(act_ref, blocks, at)


def pick_rows(own_ref, other_ref, mine_ref, theirs_ref, pick_ref, _, out_ref):
    own = (own_ref[...].astype(f32) + (mine_ref[0:128, :] + theirs_ref[128:256, :])).astype(bf16)
    other = (other_ref[0:128, :].astype(f32) + (mine_ref[128:256, :] + theirs_ref[0:128, :])).astype(bf16)
    picked = nn(pick_ref[:, 0:128], own) + nn(pick_ref[:, 128:256], other)
    out_ref[...] = picked.astype(bf16)


def interleave(rows_ref, mean, cat_ref):
    for g in range(8):
        at = slice(g * 128, g * 128 + 128)
        cat_ref[:, g * 256 : g * 256 + 128] = rows_ref[:, at]
        cat_ref[:, g * 256 + 128 : g * 256 + 256] = mean[:, at]


def layer_backward(grad, layer_ref, own_ref, mean_ref):
    for g in range(8):
        at = slice(g * 128, g * 128 + 128)
        both = nt(grad, layer_ref[g * 256 : g * 256 + 256, :])
        own_ref[:, at] = both[:, 0:128]
        mean_ref[:, at] = both[:, 128:256].astype(bf16)


def shard_rows(place_ref, offset):
    return pl.multiple_of(lax.rem(place_ref[1] + offset + 8, 8) * 256, 256)


def lay_layer(place_ref, layer, places, refs, layer_ref, sems):
    copies = []
    for half in range(2):
        side = place_ref[0] if half == 0 else 1 - place_ref[0]
        column = pl.multiple_of(side * 512, 512)
        for index, (array, start, offset) in enumerate(places):
            rows = pl.ds(shard_rows(place_ref, (1 - 2 * side) * offset), 256)
            start += layer * 256
            target = layer_ref.at[rows, pl.ds(column, 512)]
            source = refs[half][array].at[start : start + 256, :]
            copies.append(start_copy(source, target, sems.at[half * 5 + index]))
    return copies


def cotangent_part(place_ref, cot_ref, places, refs, outs):
    own_ref, mean_ref, one_ref, two_ref, one_sems, two_sems = outs
    two_copies = lay_layer(place_ref, 1, places, refs, two_ref, two_sems)
    one_copies = lay_layer(place_ref, 0, places, refs, one_ref, one_sems)
    for copy in two_copies:
        copy.wait()
    for _, _, offset in places:
        rows = shard_rows(place_ref, offset)
        at = pl.ds(pl.multiple_of(lax.rem(place_ref[1] + offset + 8, 8) * 128, 128), 128)
        both = nt(cot_ref[...], two_ref[pl.ds(rows, 256), :])
        own_ref[:, at] = both[:, 0:128]
        mean_ref[:, at] = both[:, 128:256].astype(bf16)
    return one_copies


def cotangent_near(place_ref, cot_ref, mine_ref, theirs_ref, *outs):
    places = [(0, index * 512, layer_order[index]) for index in range(5)]
    for copy in cotangent_part(place_ref, cot_ref, places, ([mine_ref], [theirs_ref]), outs):
        copy.wait()


far_starts = ((0, 2560), (1, 0), (1, 512))


def lay_far(place_ref, cot_ref, half, arrays, one_ref, two_ref):
    side = place_ref[0] if half == 0 else 1 - place_ref[0]
    column = pl.ds(pl.multiple_of(side * 512, 512), 512)
    cot = cot_ref[:, column]
    products = []
    for (array, start), offset in zip(far_starts, layer_order[5:], strict=True):
        rows = pl.ds(shard_rows(place_ref, (1 - 2 * side) * offset), 256)
        one, two = slice(start, start + 256), slice(start + 256, start + 512)
        one_ref[rows, column] = arrays[array][one, :]
        two_ref[rows, column] = arrays[array][two, :]
        products.append(nt(cot, arrays[array][two, :]))
    return products


def cotangent_far_mine(place_ref, cot_ref, near_ref, far_ref, *refs):
    one_ref, two_ref, part_ref = refs[2:]
    products = lay_far(place_ref, cot_ref, 0, (near_ref, far_ref), one_ref, two_ref)
    for index, product in enumerate(products):
        part_ref[:, index * 256 : index * 256 + 256] = product


def cotangent_far_theirs(place_ref, cot_ref, near_ref, far_ref, part_ref, count_t_ref, *refs):
    own_ref, mean_ref, one_ref, two_ref = refs[4:]
    products = lay_far(place_ref, cot_ref, 1, (near_ref, far_ref), one_ref, two_ref)
    for index, offset in enumerate(layer_order[5:]):
        both = part_ref[:, index * 256 : index * 256 + 256] + products[(1, 0, 2)[index]]
        shard = lax.rem(place_ref[1] + (1 - 2 * place_ref[0]) * offset + 8, 8)
        at = pl.ds(pl.multiple_of(shard * 128, 128), 128)
        own_ref[:, at] = both[:, 0:128]
        mean_ref[:, at] = both[:, 128:256].astype(bf16)
    own_ref[...] += nn(count_t_ref[...], mean_ref[...]) / 10.0


def graph_critical(
    in_ref, count_ref, count_t_ref, one_ref, base_ref, grad_ref, out_ref, cat_ref, own_ref, mean_ref
):
    interleave(in_ref, (nn(count_ref[...], in_ref[...]) / 10.0).astype(bf16), cat_ref)
    pre = nn(cat_ref[...], one_ref[...])
    sigmoid = 1.0 / (1.0 + jnp.exp(-pre))
    out_ref[...] = (pre * sigmoid).astype(bf16)
    pre_grad = (base_ref[...] * (sigmoid * (1.0 + pre * (1.0 - sigmoid)))).astype(bf16)
    layer_backward(pre_grad, one_ref, own_ref, mean_ref)
    spread = nn(count_t_ref[...], mean_ref[...]) / 10.0
    grad_ref[...] = (own_ref[...] + spread).astype(bf16)


def graph_output(first_ref, count_ref, two_ref, out_ref, cat_ref):
    interleave(first_ref, (nn(count_ref[...], first_ref[...]) / 10.0).astype(bf16), cat_ref)
    out_ref[...] = nn(cat_ref[...], two_ref[...]).astype(bf16)


def ff_backward(mine_ref, theirs_ref, put_mine_ref, put_theirs_ref, *refs):
    slope_refs, blocks = refs[:2], units(refs[2:-5])
    grad_ref, own_ref, other_ref, both_ref, pre_ref = refs[-5:]
    summed = nn(put_mine_ref[...], mine_ref[...]) + nn(put_theirs_ref[...], theirs_ref[...])
    both_ref[...] = summed.astype(bf16)
    grad_ref[...] = both_ref[0:128, :]
    for pair in range(8):
        late = pair >= early_blocks // 2
        start = pair * 256 - (early_blocks * 128 if late else 0)
        grown = nt(both_ref[...], out_rows(blocks, pair)) * slope_refs[late][:, start : start + 256]
        pre_ref[:, pair * 256 : pair * 256 + 256] = grown.astype(bf16)
    for column in range(0, 1024, 256):
        at = slice(column, column + 256)
        total = nn(pre_ref[:, 0:256], in_rows(blocks, 0, at))
        for pair in range(1, 8):
            total += nn(pre_ref[:, pair * 256 : pair * 256 + 256], in_rows(blocks, pair, at))
        own_ref[:, at] = total[0:128, :]
        other_ref[:, at] = total[128:256, :]


def finish(states_ref, gain_ref, grad_ref, mine_ref, theirs_ref, out_ref):
    wide = states_ref[...].astype(f32)
    inv_rms = lax.rsqrt(jnp.mean(wide * wide, axis=-1, keepdims=True) + eps_norm)
    scaled = (mine_ref[...] + theirs_ref[...]) * gain_ref[...]
    cubed = inv_rms * inv_rms * inv_rms
    result = (
        grad_ref[...].astype(f32)
        + inv_rms * scaled
        - wide * cubed * jnp.mean(scaled * wide, axis=-1, keepdims=True)
    )
    out_ref[...] = result.astype(bf16)


def on_device(
    node_states,
    norm_gain,
    w_in,
    w_out,
    self_one,
    neigh_one,
    self_two,
    neigh_two,
    send_slots,
    send_counts,
    neighbors,
    out_cotangent,
):
    gain = norm_gain.reshape(1, 1024)
    block, layer_half, place = local_call(
        prepare,
        [shape_of((256, 1024), bf16), shape_of((512, 512), bf16), shape_of((2,), jnp.int32)],
        "hhhhhh",
        "vvs",
        [pltpu.SemaphoreType.DMA((6,))],
        moved=2 << 20,
        limit=60,
    )(w_in, w_out, self_one, neigh_one, self_two, neigh_two)
    filled = jnp.arange(4, dtype=jnp.int32)[None, :] < send_counts[0][:, None]
    own_ids = jnp.where(filled, send_slots, -1).T
    (packed,) = local_call(pack, [shape_of((144, 1024), bf16)], "vv", "v", moved=1 << 20)(
        node_states, own_ids
    )
    blocks, near_parts, far_parts, other_states = gather_weights(block, layer_half, packed)
    pick_mine, put_mine, put_theirs, count, count_t = local_call(
        index_tables,
        [shape_of((128, 256), bf16)] + [shape_of((256, 128), bf16)] * 2 + [shape_of((128, 128), bf16)] * 2,
        "svvv",
        "vvvvv",
        moved=1 << 20,
    )(place, own_ids, other_states, neighbors.T)

    layer_flops = 2 * 128 * 1024 * 2048
    layer_shapes = [
        shape_of((128, 1024), f32),
        shape_of((128, 1024), bf16),
        shape_of((2048, 1024), bf16),
        shape_of((2048, 1024), bf16),
    ]
    layer_sems = [pltpu.SemaphoreType.DMA((10,))] * 2
    near = local_call(
        cotangent_near, layer_shapes, "svvv", "vvvv", layer_sems, flops=layer_flops // 2, moved=10 << 20
    )(place, out_cotangent, *near_parts)

    far = join_parts(after(far_parts[:2], far_parts, near[1]))
    far_parts = (far, swap(far))

    late_blocks = 16 - early_blocks
    block_flops = 2 * 2 * 256 * 1024 * 128
    early, slope_early, normed = local_call(
        ff_early,
        [
            shape_of((256, 1024), f32),
            shape_of((256, early_blocks * 128), f32),
            shape_of((256, 1024), bf16),
        ],
        "vvv" + "v" * (early_arrays + 1),
        "vvv",
        [pltpu.VMEM((256, early_blocks * 128), bf16)],
        flops=block_flops * early_blocks,
        moved=9 << 20,
    )(node_states, other_states, gain, *blocks[:early_arrays], count_t)
    partial, slope_late = local_call(
        ff_late,
        [shape_of((256, 1024), f32), shape_of((256, late_blocks * 128), f32)],
        "vv" + "v" * (len(blocks) - early_arrays),
        "vv",
        [pltpu.VMEM((256, late_blocks * 128), bf16)],
        flops=block_flops * late_blocks,
        moved=6 << 20,
    )(normed, early, *blocks[early_arrays:])
    partial_theirs = swap(partial)
    near_one, near_two, far_products = local_call(
        cotangent_far_mine,
        [*layer_shapes[2:], shape_of((128, 768), f32)],
        "svvvvv",
        "vvv",
        flops=layer_flops // 5,
        moved=3 << 20,
        aliases={4: 0, 5: 1},
    )(place, out_cotangent, near_parts[0], far_parts[0], *near[2:])
    base, _, layer_one, layer_two = local_call(
        cotangent_far_theirs,
        layer_shapes,
        "svvvvvvvvv",
        "vvvv",
        flops=layer_flops // 5,
        moved=4 << 20,
        aliases={6: 0, 7: 1, 8: 2, 9: 3},
    )(
        place, out_cotangent, near_parts[1], far_parts[1], far_products, count_t,
        near[0], near[1], near_one, near_two,
    )
    (outgoing,) = local_call(
        pick_rows,
        [shape_of((128, 1024), bf16)],
        "vvvvvv",
        "v",
        flops=2 * 128 * 256 * 1024,
        moved=3 << 20,
    )(node_states, other_states, partial, partial_theirs, pick_mine, base)
    incoming = lax.all_to_all(
        outgoing.reshape(16, 8, 1024), ("x", "y"), split_axis=0, concat_axis=0, tiled=True
    ).reshape(128, 1024)
    slot_grad, first_out = local_call(
        graph_critical,
        [shape_of((128, 1024), bf16), shape_of((128, 1024), bf16)],
        "vvvvv",
        "vv",
        [
            pltpu.VMEM((128, 2048), bf16),
            pltpu.VMEM((128, 1024), f32),
            pltpu.VMEM((128, 1024), bf16),
        ],
        flops=2 * layer_flops,
        moved=5 << 20,
    )(incoming, count, count_t, layer_one, base)
    returned = lax.all_to_all(
        slot_grad.reshape(16, 8, 1024), ("x", "y"), split_axis=0, concat_axis=0, tiled=True
    ).reshape(128, 1024)
    returned_theirs = swap(returned)
    embedded_grad, grad_mine, grad_other = local_call(
        ff_backward,
        [shape_of((128, 1024), bf16), shape_of((128, 1024), f32), shape_of((128, 1024), f32)],
        "vvvvvv" + "v" * len(blocks),
        "vvv",
        [pltpu.VMEM((256, 1024), bf16), pltpu.VMEM((256, 2048), bf16)],
        flops=block_flops * 16,
        moved=14 << 20,
    )(returned, returned_theirs, put_mine, put_theirs, slope_early, slope_late, *blocks)
    grad_theirs = swap(grad_other)
    (node_out,) = local_call(
        graph_output,
        [shape_of((128, 1024), bf16)],
        "vvv",
        "b",
        [pltpu.VMEM((128, 2048), bf16)],
        flops=layer_flops,
        moved=5 << 20,
    )(first_out, count, layer_two)
    (state_grad,) = local_call(
        finish, [shape_of((128, 1024), bf16)], "vvvvv", "b", moved=2 << 20
    )(node_states, gain, embedded_grad, grad_mine, grad_theirs)
    return node_out, state_grad


def solution(mesh):
    split = Mesh(mesh.devices.reshape(4, 4, 2, 8), ("x", "y", "core", "gnn"))
    lm, everywhere = ("x", "y", "core"), ("x", "y", "core", "gnn")
    rows, by_lm, by_gnn = P(everywhere, None), P(lm, None), P("gnn", None)
    return jax.shard_map(
        on_device,
        mesh=split,
        in_specs=(rows, P(), by_lm, by_lm, by_gnn, by_gnn, by_gnn, by_gnn, rows, rows, rows, rows),
        out_specs=(rows, rows),
        check_vma=False,
    )
```

```python
import jax
import jax.numpy as jnp
from jax import lax
from jax.experimental import pallas as pl
from jax.experimental.pallas import tpu as pltpu
from jax.sharding import Mesh
from jax.sharding import PartitionSpec as P

eps_norm = 1e-06
root_coef = 0.7978845608028654
cubic_coef = 0.044715
f32 = jnp.float32
bf16 = jnp.bfloat16

layer_order = (0, -1, 1, -2, 2, -3, 3, -4)
early_arrays = 3
early_blocks = 12


def nt(left, right):
    return lax.dot_general(left, right, (((1,), (1,)), ((), ())), preferred_element_type=f32)


def nn(left, right):
    return jnp.dot(left, right, preferred_element_type=f32)


def local_call(kernel, out_shape, ins, outs, scratch=(), flops=0, moved=0, limit=10, aliases=None):
    specs = {
        "v": pl.BlockSpec(memory_space=pltpu.VMEM),
        "s": pl.BlockSpec(memory_space=pltpu.SMEM),
        "b": pl.BlockSpec(),
        "h": pl.BlockSpec(memory_space=pltpu.HBM),
    }
    return pl.pallas_call(
        kernel,
        out_shape=out_shape,
        in_specs=[specs[kind] for kind in ins],
        out_specs=[specs[kind] for kind in outs],
        scratch_shapes=list(scratch),
        input_output_aliases=aliases or {},
        compiler_params=pltpu.CompilerParams(vmem_limit_bytes=limit * 1024 * 1024),
        cost_estimate=pl.CostEstimate(flops=flops, bytes_accessed=moved, transcendentals=0),
    )


def shape_of(dims, dtype):
    return jax.ShapeDtypeStruct(dims, dtype)


def swap(values):
    return lax.ppermute(values, "core", [(0, 1), (1, 0)])


def shift_plane(values, phase, step):
    pairs = []
    for x in range(4):
        for y in range(4):
            for c in range(2):
                along_x = (phase == 1) == (c == 0)
                to = ((x + step) % 4, y) if along_x else (x, (y + step) % 4)
                pairs.append(((x * 4 + y) * 2 + c, (to[0] * 4 + to[1]) * 2 + c))
    return lax.ppermute(values, ("x", "y", "core"), pairs)


def shift_first(values, step):
    return shift_plane(values, 1, step)


def shift_second(values, step):
    return shift_plane(values, 2, step)


def after(values, *others):
    return lax.optimization_barrier((values, others))[0]


def gather_weights(block, part, states):
    right_1, left_1 = shift_ring(part, 1), shift_ring(part, -1)
    ahead, behind, opposite = shift_first(block, 1), shift_first(block, -1), shift_first(block, 2)
    other_states = swap(states)
    line = fill_line(open_line(block), ahead, behind, opposite)

    first = (right_1, left_1, ahead, behind, opposite, other_states)
    right_2 = shift_ring(after(right_1, first), 1)
    left_2 = shift_ring(after(left_1, first), -1)
    right_3 = shift_ring(after(right_1, first), 2)
    line = after(line, first)
    up, down = shift_second(line, 1), shift_second(line, -1)

    second = (right_2, left_2, right_3, up, down)
    left_3 = shift_ring(after(left_2, second), -1)
    right_4 = shift_ring(after(right_3, second), 1)
    far_up = shift_second(after(cut_rows(up, 0), second), 1)
    far_down = shift_second(after(cut_rows(down, 512), second), -1)
    near = join_parts(after([part, right_1, left_1, right_2, left_2, right_3], second))
    near_theirs = swap(near)

    far = [left_3, right_4, far_up, far_down]
    return [line, up, down, far_up, far_down], (near, near_theirs), far, other_states


def shift_ring(values, step):
    pairs = [
        (c * 8 + g, c * 8 + (g + (step if c == 0 else -step)) % 8) for c in range(2) for g in range(8)
    ]
    return lax.ppermute(values, ("core", "gnn"), pairs)


def start_copy(source, target, sem):
    copy = pltpu.make_async_copy(source, target, sem)
    copy.start()
    return copy


def prepare(in_ref, out_ref, *refs):
    block_ref, half_ref, place_ref, sems = refs[4:]
    core = lax.axis_index("core")
    columns = pl.ds(pl.multiple_of(core * 512, 512), 512)
    copies = [
        start_copy(in_ref, block_ref.at[0:128, :], sems.at[0]),
        start_copy(out_ref, block_ref.at[128:256, :], sems.at[1]),
    ]
    for index in range(4):
        target = half_ref.at[index * 128 : index * 128 + 128, :]
        copies.append(start_copy(refs[index].at[:, columns], target, sems.at[2 + index]))
    place_ref[0] = core
    place_ref[1] = lax.axis_index("gnn")
    for copy in copies:
        copy.wait()


def join(*refs):
    rows = refs[0].shape[0]
    for index, ref in enumerate(refs[:-1]):
        refs[-1][index * rows : index * rows + rows, :] = ref[...]


def pack(states_ref, ids_ref, out_ref):
    out_ref[0:128, :] = states_ref[...]
    out_ref[128:144, :] = jnp.zeros((16, 1024), bf16)
    ids = ids_ref[...].astype(f32).astype(bf16)
    rows = (lax.broadcasted_iota(jnp.int32, (16, 4), 0) == lax.broadcasted_iota(jnp.int32, (16, 4), 1)).astype(bf16)
    columns = (lax.broadcasted_iota(jnp.int32, (32, 128), 0) == lax.broadcasted_iota(jnp.int32, (32, 128), 1)).astype(bf16)
    out_ref[128:144, 0:128] = nn(nn(rows, ids).astype(bf16), columns).astype(bf16)


def join_parts(parts):
    rows, columns = parts[0].shape
    (whole,) = local_call(
        join,
        [shape_of((len(parts) * rows, columns), bf16)],
        "v" * len(parts),
        "v",
        moved=len(parts) << 20,
    )(*parts)
    return whole


def cut_rows(values, start):
    def cut(ref, out_ref):
        out_ref[...] = ref[start : start + 512, :]

    (rows,) = local_call(cut, [shape_of((512, 1024), bf16)], "v", "v", moved=2 << 20)(values)
    return rows


def open_line(block):
    def open_up(ref, out_ref):
        out_ref[0:256, :] = ref[...]

    (line,) = local_call(open_up, [shape_of((1024, 1024), bf16)], "v", "v", moved=1 << 20)(block)
    return line


def fill_line(line, *blocks):
    def fill(_, *refs):
        for index, ref in enumerate(refs[:-1]):
            refs[-1][index * 256 + 256 : index * 256 + 512, :] = ref[...]

    (line,) = local_call(
        fill, [shape_of((1024, 1024), bf16)], "vvvv", "v", moved=3 << 20, aliases={0: 0}
    )(line, *blocks)
    return line


def transposed(left, eye):
    return lax.dot_general(left, eye, (((0,), (0,)), ((), ())), preferred_element_type=f32)


def index_tables(place_ref, own_ref, other_ref, neighbors_ref, *refs):
    pick_mine_ref, put_mine_ref, put_theirs_ref, count_ref, count_t_ref = refs
    core = place_ref[0]

    def iota(rows, columns, axis):
        return lax.broadcasted_iota(jnp.int32, (rows, columns), axis)

    eye = (iota(128, 128, 0) == iota(128, 128, 1)).astype(bf16)
    own, other = own_ref[...].astype(f32).astype(bf16), other_ref[128:144, 0:128][0:4, 0:32]
    slot = iota(128, 4, 0) & 3 == iota(128, 4, 1)
    side = (iota(128, 1, 0) >> 2) & 1

    def pick(worker):
        rows = (iota(128, 32, 1) == (iota(128, 32, 0) >> 3) * 2 + worker).astype(bf16)
        own_id = jnp.sum(jnp.where(slot, nt(rows, own), 0.0), axis=1, keepdims=True)
        other_id = jnp.sum(jnp.where(slot, nt(rows, other), 0.0), axis=1, keepdims=True)
        other_id = jnp.where(other_id < 0.0, -1.0, other_id + 128.0)
        ids = jnp.where(side == core, own_id, other_id).astype(jnp.int32)
        return (ids == iota(128, 256, 1)).astype(bf16)

    mine = pick(core)
    pick_mine_ref[...] = mine
    put_mine_ref[...] = transposed(mine, eye).astype(bf16)
    put_theirs_ref[...] = transposed(pick(1 - core), eye).astype(bf16)
    count_t = jnp.zeros((128, 128), f32)
    for index in range(neighbors_ref.shape[0]):
        count_t += (neighbors_ref[index : index + 1, :] == iota(128, 128, 0)).astype(f32)
    count_t = count_t.astype(bf16)
    count_t_ref[...] = count_t
    count_ref[...] = transposed(count_t, eye).astype(bf16)


def units(refs):
    return [(ref, start) for ref in refs for start in range(0, ref.shape[0], 256)]


def in_rows(blocks, pair, at=slice(None)):
    return jnp.concatenate([ref[s : s + 128, at] for ref, s in blocks[2 * pair : 2 * pair + 2]], axis=0)


def out_rows(blocks, pair, at=slice(None)):
    return jnp.concatenate([ref[s + 128 : s + 256, at] for ref, s in blocks[2 * pair : 2 * pair + 2]], axis=0)


def expand_blocks(normed_ref, blocks, slope_ref, act_ref):
    for pair in range(len(blocks) // 2):
        pre = nt(normed_ref[...], in_rows(blocks, pair))
        square = pre * pre
        tangent = jnp.tanh(root_coef * (pre + cubic_coef * square * pre))
        at = slice(pair * 256, pair * 256 + 256)
        act_ref[:, at] = (0.5 * pre * (1.0 + tangent)).astype(bf16)
        slope_ref[:, at] = 0.5 * (1.0 + tangent) + 0.5 * pre * (
            1.0 - tangent * tangent
        ) * root_coef * (1.0 + 3.0 * cubic_coef * square)


def contract_blocks(act_ref, blocks, at):
    total = nn(act_ref[:, 0:256], out_rows(blocks, 0, at))
    for pair in range(1, len(blocks) // 2):
        total += nn(act_ref[:, pair * 256 : pair * 256 + 256], out_rows(blocks, pair, at))
    return total


def ff_early(own_ref, other_ref, gain_ref, *refs):
    blocks = units(refs[:early_arrays])
    partial_ref, slope_ref, normed_ref, act_ref = refs[-4:]
    for part, ref in enumerate((own_ref, other_ref)):
        wide = ref[0:128, :].astype(f32)
        inv_rms = lax.rsqrt(jnp.mean(wide * wide, axis=-1, keepdims=True) + eps_norm)
        normed_ref[part * 128 : part * 128 + 128, :] = (wide * inv_rms * gain_ref[...]).astype(bf16)
    expand_blocks(normed_ref, blocks, slope_ref, act_ref)
    for column in range(0, 1024, 256):
        at = slice(column, column + 256)
        partial_ref[:, at] = contract_blocks(act_ref, blocks, at)


def ff_late(normed_ref, early_ref, *refs):
    partial_ref, slope_ref, act_ref = refs[-3:]
    blocks = units(refs[:-3])
    expand_blocks(normed_ref, blocks, slope_ref, act_ref)
    for column in range(0, 1024, 256):
        at = slice(column, column + 256)
        partial_ref[:, at] = early_ref[:, at] + contract_blocks(act_ref, blocks, at)


def pick_rows(own_ref, other_ref, mine_ref, theirs_ref, pick_ref, _, out_ref):
    own = (own_ref[...].astype(f32) + (mine_ref[0:128, :] + theirs_ref[128:256, :])).astype(bf16)
    other = (other_ref[0:128, :].astype(f32) + (mine_ref[128:256, :] + theirs_ref[0:128, :])).astype(bf16)
    picked = nn(pick_ref[:, 0:128], own) + nn(pick_ref[:, 128:256], other)
    out_ref[...] = picked.astype(bf16)


def interleave(rows_ref, mean, cat_ref):
    for g in range(8):
        at = slice(g * 128, g * 128 + 128)
        cat_ref[:, g * 256 : g * 256 + 128] = rows_ref[:, at]
        cat_ref[:, g * 256 + 128 : g * 256 + 256] = mean[:, at]


def layer_backward(grad, layer_ref, own_ref, mean_ref):
    for g in range(8):
        at = slice(g * 128, g * 128 + 128)
        both = nt(grad, layer_ref[g * 256 : g * 256 + 256, :])
        own_ref[:, at] = both[:, 0:128]
        mean_ref[:, at] = both[:, 128:256].astype(bf16)


def shard_rows(place_ref, offset):
    return pl.multiple_of(lax.rem(place_ref[1] + offset + 8, 8) * 256, 256)


def lay_layer(place_ref, layer, places, refs, layer_ref, sems):
    copies = []
    for half in range(2):
        side = place_ref[0] if half == 0 else 1 - place_ref[0]
        column = pl.multiple_of(side * 512, 512)
        for index, (array, start, offset) in enumerate(places):
            rows = pl.ds(shard_rows(place_ref, (1 - 2 * side) * offset), 256)
            start += layer * 256
            target = layer_ref.at[rows, pl.ds(column, 512)]
            source = refs[half][array].at[start : start + 256, :]
            copies.append(start_copy(source, target, sems.at[half * 5 + index]))
    return copies


def cotangent_part(place_ref, cot_ref, places, refs, outs):
    own_ref, mean_ref, one_ref, two_ref, one_sems, two_sems = outs
    two_copies = lay_layer(place_ref, 1, places, refs, two_ref, two_sems)
    one_copies = lay_layer(place_ref, 0, places, refs, one_ref, one_sems)
    for copy in two_copies:
        copy.wait()
    for _, _, offset in places:
        rows = shard_rows(place_ref, offset)
        at = pl.ds(pl.multiple_of(lax.rem(place_ref[1] + offset + 8, 8) * 128, 128), 128)
        both = nt(cot_ref[...], two_ref[pl.ds(rows, 256), :])
        own_ref[:, at] = both[:, 0:128]
        mean_ref[:, at] = both[:, 128:256].astype(bf16)
    return one_copies


def cotangent_near(place_ref, cot_ref, mine_ref, theirs_ref, *outs):
    places = [(0, index * 512, layer_order[index]) for index in range(5)]
    for copy in cotangent_part(place_ref, cot_ref, places, ([mine_ref], [theirs_ref]), outs):
        copy.wait()


far_starts = ((0, 2560), (1, 0), (1, 512))


def lay_far(place_ref, cot_ref, half, arrays, one_ref, two_ref):
    side = place_ref[0] if half == 0 else 1 - place_ref[0]
    column = pl.ds(pl.multiple_of(side * 512, 512), 512)
    cot = cot_ref[:, column]
    products = []
    for (array, start), offset in zip(far_starts, layer_order[5:], strict=True):
        rows = pl.ds(shard_rows(place_ref, (1 - 2 * side) * offset), 256)
        one, two = slice(start, start + 256), slice(start + 256, start + 512)
        one_ref[rows, column] = arrays[array][one, :]
        two_ref[rows, column] = arrays[array][two, :]
        products.append(nt(cot, arrays[array][two, :]))
    return products


def cotangent_far_mine(place_ref, cot_ref, near_ref, far_ref, *refs):
    one_ref, two_ref, part_ref = refs[2:]
    products = lay_far(place_ref, cot_ref, 0, (near_ref, far_ref), one_ref, two_ref)
    for index, product in enumerate(products):
        part_ref[:, index * 256 : index * 256 + 256] = product


def cotangent_far_theirs(place_ref, cot_ref, near_ref, far_ref, part_ref, count_t_ref, *refs):
    own_ref, mean_ref, one_ref, two_ref = refs[4:]
    products = lay_far(place_ref, cot_ref, 1, (near_ref, far_ref), one_ref, two_ref)
    for index, offset in enumerate(layer_order[5:]):
        both = part_ref[:, index * 256 : index * 256 + 256] + products[(1, 0, 2)[index]]
        shard = lax.rem(place_ref[1] + (1 - 2 * place_ref[0]) * offset + 8, 8)
        at = pl.ds(pl.multiple_of(shard * 128, 128), 128)
        own_ref[:, at] = both[:, 0:128]
        mean_ref[:, at] = both[:, 128:256].astype(bf16)
    own_ref[...] += nn(count_t_ref[...], mean_ref[...]) / 10.0


def graph_critical(
    in_ref, count_ref, count_t_ref, one_ref, base_ref, grad_ref, out_ref, cat_ref, own_ref, mean_ref
):
    interleave(in_ref, (nn(count_ref[...], in_ref[...]) / 10.0).astype(bf16), cat_ref)
    for column in range(0, 1024, 256):
        at = slice(column, column + 256)
        pre = nn(cat_ref[...], one_ref[:, at])
        sigmoid = 1.0 / (1.0 + jnp.exp(-pre))
        out_ref[:, at] = (pre * sigmoid).astype(bf16)
        slope = sigmoid * (1.0 + pre * (1.0 - sigmoid))
        grad_ref[:, at] = (base_ref[:, at] * slope).astype(bf16)
    layer_backward(grad_ref[...], one_ref, own_ref, mean_ref)
    for column in range(0, 1024, 256):
        at = slice(column, column + 256)
        spread = nn(count_t_ref[...], mean_ref[:, at]) / 10.0
        grad_ref[:, at] = (own_ref[:, at] + spread).astype(bf16)


def graph_output(first_ref, count_ref, two_ref, out_ref, cat_ref):
    interleave(first_ref, (nn(count_ref[...], first_ref[...]) / 10.0).astype(bf16), cat_ref)
    out_ref[...] = nn(cat_ref[...], two_ref[...]).astype(bf16)


def ff_backward(mine_ref, theirs_ref, put_mine_ref, put_theirs_ref, *refs):
    slope_refs, blocks = refs[:2], units(refs[2:-5])
    grad_ref, own_ref, other_ref, both_ref, pre_ref = refs[-5:]
    summed = nn(put_mine_ref[...], mine_ref[...]) + nn(put_theirs_ref[...], theirs_ref[...])
    both_ref[...] = summed.astype(bf16)
    grad_ref[...] = both_ref[0:128, :]
    for pair in range(8):
        late = pair >= early_blocks // 2
        start = pair * 256 - (early_blocks * 128 if late else 0)
        grown = nt(both_ref[...], out_rows(blocks, pair)) * slope_refs[late][:, start : start + 256]
        pre_ref[:, pair * 256 : pair * 256 + 256] = grown.astype(bf16)
    for column in range(0, 1024, 256):
        at = slice(column, column + 256)
        total = nn(pre_ref[:, 0:256], in_rows(blocks, 0, at))
        for pair in range(1, 8):
            total += nn(pre_ref[:, pair * 256 : pair * 256 + 256], in_rows(blocks, pair, at))
        own_ref[:, at] = total[0:128, :]
        other_ref[:, at] = total[128:256, :]


def finish(states_ref, gain_ref, grad_ref, mine_ref, theirs_ref, out_ref):
    wide = states_ref[...].astype(f32)
    inv_rms = lax.rsqrt(jnp.mean(wide * wide, axis=-1, keepdims=True) + eps_norm)
    scaled = (mine_ref[...] + theirs_ref[...]) * gain_ref[...]
    cubed = inv_rms * inv_rms * inv_rms
    result = (
        grad_ref[...].astype(f32)
        + inv_rms * scaled
        - wide * cubed * jnp.mean(scaled * wide, axis=-1, keepdims=True)
    )
    out_ref[...] = result.astype(bf16)


def on_device(
    node_states,
    norm_gain,
    w_in,
    w_out,
    self_one,
    neigh_one,
    self_two,
    neigh_two,
    send_slots,
    send_counts,
    neighbors,
    out_cotangent,
):
    gain = norm_gain.reshape(1, 1024)
    block, layer_half, place = local_call(
        prepare,
        [shape_of((256, 1024), bf16), shape_of((512, 512), bf16), shape_of((2,), jnp.int32)],
        "hhhhhh",
        "vvs",
        [pltpu.SemaphoreType.DMA((6,))],
        moved=2 << 20,
        limit=60,
    )(w_in, w_out, self_one, neigh_one, self_two, neigh_two)
    filled = jnp.arange(4, dtype=jnp.int32)[None, :] < send_counts[0][:, None]
    own_ids = jnp.where(filled, send_slots, -1).T
    (packed,) = local_call(pack, [shape_of((144, 1024), bf16)], "vv", "v", moved=1 << 20)(
        node_states, own_ids
    )
    blocks, near_parts, far_parts, other_states = gather_weights(block, layer_half, packed)
    pick_mine, put_mine, put_theirs, count, count_t = local_call(
        index_tables,
        [shape_of((128, 256), bf16)] + [shape_of((256, 128), bf16)] * 2 + [shape_of((128, 128), bf16)] * 2,
        "svvv",
        "vvvvv",
        moved=1 << 20,
    )(place, own_ids, other_states, neighbors.T)

    layer_flops = 2 * 128 * 1024 * 2048
    layer_shapes = [
        shape_of((128, 1024), f32),
        shape_of((128, 1024), bf16),
        shape_of((2048, 1024), bf16),
        shape_of((2048, 1024), bf16),
    ]
    layer_sems = [pltpu.SemaphoreType.DMA((10,))] * 2
    near = local_call(
        cotangent_near, layer_shapes, "svvv", "vvvv", layer_sems, flops=layer_flops // 2, moved=10 << 20
    )(place, out_cotangent, *near_parts)

    far = join_parts(after(far_parts[:2], far_parts, near[1]))
    far_parts = (far, swap(far))

    late_blocks = 16 - early_blocks
    block_flops = 2 * 2 * 256 * 1024 * 128
    early, slope_early, normed = local_call(
        ff_early,
        [
            shape_of((256, 1024), f32),
            shape_of((256, early_blocks * 128), f32),
            shape_of((256, 1024), bf16),
        ],
        "vvv" + "v" * (early_arrays + 1),
        "vvv",
        [pltpu.VMEM((256, early_blocks * 128), bf16)],
        flops=block_flops * early_blocks,
        moved=9 << 20,
    )(node_states, other_states, gain, *blocks[:early_arrays], count_t)
    partial, slope_late = local_call(
        ff_late,
        [shape_of((256, 1024), f32), shape_of((256, late_blocks * 128), f32)],
        "vv" + "v" * (len(blocks) - early_arrays),
        "vv",
        [pltpu.VMEM((256, late_blocks * 128), bf16)],
        flops=block_flops * late_blocks,
        moved=6 << 20,
    )(normed, early, *blocks[early_arrays:])
    partial_theirs = swap(partial)
    near_one, near_two, far_products = local_call(
        cotangent_far_mine,
        [*layer_shapes[2:], shape_of((128, 768), f32)],
        "svvvvv",
        "vvv",
        flops=layer_flops // 5,
        moved=3 << 20,
        aliases={4: 0, 5: 1},
    )(place, out_cotangent, near_parts[0], far_parts[0], *near[2:])
    base, _, layer_one, layer_two = local_call(
        cotangent_far_theirs,
        layer_shapes,
        "svvvvvvvvv",
        "vvvv",
        flops=layer_flops // 5,
        moved=4 << 20,
        aliases={6: 0, 7: 1, 8: 2, 9: 3},
    )(
        place, out_cotangent, near_parts[1], far_parts[1], far_products, count_t,
        near[0], near[1], near_one, near_two,
    )
    (outgoing,) = local_call(
        pick_rows,
        [shape_of((128, 1024), bf16)],
        "vvvvvv",
        "v",
        flops=2 * 128 * 256 * 1024,
        moved=3 << 20,
    )(node_states, other_states, partial, partial_theirs, pick_mine, base)
    incoming = lax.all_to_all(
        outgoing.reshape(16, 8, 1024), ("x", "y"), split_axis=0, concat_axis=0, tiled=True
    ).reshape(128, 1024)
    slot_grad, first_out = local_call(
        graph_critical,
        [shape_of((128, 1024), bf16), shape_of((128, 1024), bf16)],
        "vvvvv",
        "vv",
        [
            pltpu.VMEM((128, 2048), bf16),
            pltpu.VMEM((128, 1024), f32),
            pltpu.VMEM((128, 1024), bf16),
        ],
        flops=2 * layer_flops,
        moved=5 << 20,
    )(incoming, count, count_t, layer_one, base)
    returned = lax.all_to_all(
        slot_grad.reshape(16, 8, 1024), ("x", "y"), split_axis=0, concat_axis=0, tiled=True
    ).reshape(128, 1024)
    returned_theirs = swap(returned)
    embedded_grad, grad_mine, grad_other = local_call(
        ff_backward,
        [shape_of((128, 1024), bf16), shape_of((128, 1024), f32), shape_of((128, 1024), f32)],
        "vvvvvv" + "v" * len(blocks),
        "vvv",
        [pltpu.VMEM((256, 1024), bf16), pltpu.VMEM((256, 2048), bf16)],
        flops=block_flops * 16,
        moved=14 << 20,
    )(returned, returned_theirs, put_mine, put_theirs, slope_early, slope_late, *blocks)
    grad_theirs = swap(grad_other)
    (node_out,) = local_call(
        graph_output,
        [shape_of((128, 1024), bf16)],
        "vvv",
        "b",
        [pltpu.VMEM((128, 2048), bf16)],
        flops=layer_flops,
        moved=5 << 20,
    )(first_out, count, layer_two)
    (state_grad,) = local_call(
        finish, [shape_of((128, 1024), bf16)], "vvvvv", "b", moved=2 << 20
    )(node_states, gain, embedded_grad, grad_mine, grad_theirs)
    return node_out, state_grad


def solution(mesh):
    split = Mesh(mesh.devices.reshape(4, 4, 2, 8), ("x", "y", "core", "gnn"))
    lm, everywhere = ("x", "y", "core"), ("x", "y", "core", "gnn")
    rows, by_lm, by_gnn = P(everywhere, None), P(lm, None), P("gnn", None)
    return jax.shard_map(
        on_device,
        mesh=split,
        in_specs=(rows, P(), by_lm, by_lm, by_gnn, by_gnn, by_gnn, by_gnn, rows, rows, rows, rows),
        out_specs=(rows, rows),
        check_vma=False,
    )
```

```python
import jax
import jax.numpy as jnp
from jax import lax
from jax.experimental import pallas as pl
from jax.experimental.pallas import tpu as pltpu
from jax.sharding import Mesh
from jax.sharding import PartitionSpec as P

eps_norm = 1e-06
root_coef = 0.7978845608028654
cubic_coef = 0.044715
f32 = jnp.float32
bf16 = jnp.bfloat16

layer_order = (0, -1, 1, -2, 2, -3, 3, -4)
early_arrays = 3
early_blocks = 12


def nt(left, right):
    return lax.dot_general(left, right, (((1,), (1,)), ((), ())), preferred_element_type=f32)


def nn(left, right):
    return jnp.dot(left, right, preferred_element_type=f32)


def local_call(kernel, out_shape, ins, outs, scratch=(), flops=0, moved=0, limit=10, aliases=None):
    specs = {
        "v": pl.BlockSpec(memory_space=pltpu.VMEM),
        "s": pl.BlockSpec(memory_space=pltpu.SMEM),
        "b": pl.BlockSpec(),
        "h": pl.BlockSpec(memory_space=pltpu.HBM),
    }
    return pl.pallas_call(
        kernel,
        out_shape=out_shape,
        in_specs=[specs[kind] for kind in ins],
        out_specs=[specs[kind] for kind in outs],
        scratch_shapes=list(scratch),
        input_output_aliases=aliases or {},
        compiler_params=pltpu.CompilerParams(vmem_limit_bytes=limit * 1024 * 1024),
        cost_estimate=pl.CostEstimate(flops=flops, bytes_accessed=moved, transcendentals=0),
    )


def shape_of(dims, dtype):
    return jax.ShapeDtypeStruct(dims, dtype)


def swap(values):
    return lax.ppermute(values, "core", [(0, 1), (1, 0)])


def shift_plane(values, phase, step):
    pairs = []
    for x in range(4):
        for y in range(4):
            for c in range(2):
                along_x = (phase == 1) == (c == 0)
                to = ((x + step) % 4, y) if along_x else (x, (y + step) % 4)
                pairs.append(((x * 4 + y) * 2 + c, (to[0] * 4 + to[1]) * 2 + c))
    return lax.ppermute(values, ("x", "y", "core"), pairs)


def shift_first(values, step):
    return shift_plane(values, 1, step)


def shift_second(values, step):
    return shift_plane(values, 2, step)


def after(values, *others):
    return lax.optimization_barrier((values, others))[0]


def gather_weights(block, part, states):
    right_1, left_1 = shift_ring(part, 1), shift_ring(part, -1)
    ahead, behind, opposite = shift_first(block, 1), shift_first(block, -1), shift_first(block, 2)
    other_states = swap(states)
    line = fill_line(open_line(block), ahead, behind, opposite)

    first = (right_1, left_1, ahead, behind, opposite, other_states)
    right_2 = shift_ring(after(right_1, first), 1)
    left_2 = shift_ring(after(left_1, first), -1)
    right_3 = shift_ring(after(right_1, first), 2)
    line = after(line, first)
    up, down = shift_second(line, 1), shift_second(line, -1)

    second = (right_2, left_2, right_3, up, down)
    left_3 = shift_ring(after(left_2, second), -1)
    right_4 = shift_ring(after(right_3, second), 1)
    far_up = shift_second(after(cut_rows(up, 0), second), 1)
    far_down = shift_second(after(cut_rows(down, 512), second), -1)
    near = join_parts(after([part, right_1, left_1, right_2, left_2, right_3], second))
    near_theirs = swap(near)

    far = [left_3, right_4, far_up, far_down]
    return [line, up, down, far_up, far_down], (near, near_theirs), far, other_states


def shift_ring(values, step):
    pairs = [
        (c * 8 + g, c * 8 + (g + (step if c == 0 else -step)) % 8) for c in range(2) for g in range(8)
    ]
    return lax.ppermute(values, ("core", "gnn"), pairs)


def start_copy(source, target, sem):
    copy = pltpu.make_async_copy(source, target, sem)
    copy.start()
    return copy


def prepare(in_ref, out_ref, *refs):
    block_ref, half_ref, place_ref, sems = refs[4:]
    core = lax.axis_index("core")
    columns = pl.ds(pl.multiple_of(core * 512, 512), 512)
    copies = [
        start_copy(in_ref, block_ref.at[0:128, :], sems.at[0]),
        start_copy(out_ref, block_ref.at[128:256, :], sems.at[1]),
    ]
    for index in range(4):
        target = half_ref.at[index * 128 : index * 128 + 128, :]
        copies.append(start_copy(refs[index].at[:, columns], target, sems.at[2 + index]))
    place_ref[0] = core
    place_ref[1] = lax.axis_index("gnn")
    for copy in copies:
        copy.wait()


def join(*refs):
    rows = refs[0].shape[0]
    for index, ref in enumerate(refs[:-1]):
        refs[-1][index * rows : index * rows + rows, :] = ref[...]


def pack(states_ref, ids_ref, out_ref):
    out_ref[0:128, :] = states_ref[...]
    out_ref[128:144, :] = jnp.zeros((16, 1024), bf16)
    ids = ids_ref[...].astype(f32).astype(bf16)
    rows = (lax.broadcasted_iota(jnp.int32, (16, 4), 0) == lax.broadcasted_iota(jnp.int32, (16, 4), 1)).astype(bf16)
    columns = (lax.broadcasted_iota(jnp.int32, (32, 128), 0) == lax.broadcasted_iota(jnp.int32, (32, 128), 1)).astype(bf16)
    out_ref[128:144, 0:128] = nn(nn(rows, ids).astype(bf16), columns).astype(bf16)


def join_parts(parts):
    rows, columns = parts[0].shape
    (whole,) = local_call(
        join,
        [shape_of((len(parts) * rows, columns), bf16)],
        "v" * len(parts),
        "v",
        moved=len(parts) << 20,
    )(*parts)
    return whole


def cut_rows(values, start):
    def cut(ref, out_ref):
        out_ref[...] = ref[start : start + 512, :]

    (rows,) = local_call(cut, [shape_of((512, 1024), bf16)], "v", "v", moved=2 << 20)(values)
    return rows


def open_line(block):
    def open_up(ref, out_ref):
        out_ref[0:256, :] = ref[...]

    (line,) = local_call(open_up, [shape_of((1024, 1024), bf16)], "v", "v", moved=1 << 20)(block)
    return line


def fill_line(line, *blocks):
    def fill(_, *refs):
        for index, ref in enumerate(refs[:-1]):
            refs[-1][index * 256 + 256 : index * 256 + 512, :] = ref[...]

    (line,) = local_call(
        fill, [shape_of((1024, 1024), bf16)], "vvvv", "v", moved=3 << 20, aliases={0: 0}
    )(line, *blocks)
    return line


def transposed(left, eye):
    return lax.dot_general(left, eye, (((0,), (0,)), ((), ())), preferred_element_type=f32)


def index_tables(place_ref, own_ref, other_ref, neighbors_ref, *refs):
    pick_mine_ref, put_mine_ref, put_theirs_ref, count_ref, count_t_ref = refs
    core = place_ref[0]

    def iota(rows, columns, axis):
        return lax.broadcasted_iota(jnp.int32, (rows, columns), axis)

    eye = (iota(128, 128, 0) == iota(128, 128, 1)).astype(bf16)
    own, other = own_ref[...].astype(f32).astype(bf16), other_ref[128:144, 0:128][0:4, 0:32]
    slot = iota(128, 4, 0) & 3 == iota(128, 4, 1)
    side = (iota(128, 1, 0) >> 2) & 1

    def pick(worker):
        rows = (iota(128, 32, 1) == (iota(128, 32, 0) >> 3) * 2 + worker).astype(bf16)
        own_id = jnp.sum(jnp.where(slot, nt(rows, own), 0.0), axis=1, keepdims=True)
        other_id = jnp.sum(jnp.where(slot, nt(rows, other), 0.0), axis=1, keepdims=True)
        other_id = jnp.where(other_id < 0.0, -1.0, other_id + 128.0)
        ids = jnp.where(side == core, own_id, other_id).astype(jnp.int32)
        return (ids == iota(128, 256, 1)).astype(bf16)

    mine = pick(core)
    pick_mine_ref[...] = mine
    put_mine_ref[...] = transposed(mine, eye).astype(bf16)
    put_theirs_ref[...] = transposed(pick(1 - core), eye).astype(bf16)
    count_t = jnp.zeros((128, 128), f32)
    for index in range(neighbors_ref.shape[0]):
        count_t += (neighbors_ref[index : index + 1, :] == iota(128, 128, 0)).astype(f32)
    count_t = count_t.astype(bf16)
    count_t_ref[...] = count_t
    count_ref[...] = transposed(count_t, eye).astype(bf16)


def units(refs):
    return [(ref, start) for ref in refs for start in range(0, ref.shape[0], 256)]


def in_rows(blocks, pair, at=slice(None)):
    return jnp.concatenate([ref[s : s + 128, at] for ref, s in blocks[2 * pair : 2 * pair + 2]], axis=0)


def out_rows(blocks, pair, at=slice(None)):
    return jnp.concatenate([ref[s + 128 : s + 256, at] for ref, s in blocks[2 * pair : 2 * pair + 2]], axis=0)


def expand_blocks(normed_ref, blocks, slope_ref, act_ref):
    for pair in range(len(blocks) // 2):
        pre = nt(normed_ref[...], in_rows(blocks, pair))
        square = pre * pre
        tangent = jnp.tanh(root_coef * (pre + cubic_coef * square * pre))
        at = slice(pair * 256, pair * 256 + 256)
        act_ref[:, at] = (0.5 * pre * (1.0 + tangent)).astype(bf16)
        slope_ref[:, at] = 0.5 * (1.0 + tangent) + 0.5 * pre * (
            1.0 - tangent * tangent
        ) * root_coef * (1.0 + 3.0 * cubic_coef * square)


def contract_blocks(act_ref, blocks, at):
    total = nn(act_ref[:, 0:256], out_rows(blocks, 0, at))
    for pair in range(1, len(blocks) // 2):
        total += nn(act_ref[:, pair * 256 : pair * 256 + 256], out_rows(blocks, pair, at))
    return total


def ff_early(own_ref, other_ref, gain_ref, *refs):
    blocks = units(refs[:early_arrays])
    partial_ref, slope_ref, normed_ref, act_ref = refs[-4:]
    for part, ref in enumerate((own_ref, other_ref)):
        wide = ref[0:128, :].astype(f32)
        inv_rms = lax.rsqrt(jnp.mean(wide * wide, axis=-1, keepdims=True) + eps_norm)
        normed_ref[part * 128 : part * 128 + 128, :] = (wide * inv_rms * gain_ref[...]).astype(bf16)
    expand_blocks(normed_ref, blocks, slope_ref, act_ref)
    for column in range(0, 1024, 256):
        at = slice(column, column + 256)
        partial_ref[:, at] = contract_blocks(act_ref, blocks, at)


def ff_late(normed_ref, early_ref, *refs):
    partial_ref, slope_ref, act_ref = refs[-3:]
    blocks = units(refs[:-3])
    expand_blocks(normed_ref, blocks, slope_ref, act_ref)
    for column in range(0, 1024, 256):
        at = slice(column, column + 256)
        partial_ref[:, at] = early_ref[:, at] + contract_blocks(act_ref, blocks, at)


def pick_rows(own_ref, other_ref, mine_ref, theirs_ref, pick_ref, _, out_ref):
    own = (own_ref[...].astype(f32) + (mine_ref[0:128, :] + theirs_ref[128:256, :])).astype(bf16)
    other = (other_ref[0:128, :].astype(f32) + (mine_ref[128:256, :] + theirs_ref[0:128, :])).astype(bf16)
    picked = nn(pick_ref[:, 0:128], own) + nn(pick_ref[:, 128:256], other)
    out_ref[...] = picked.astype(bf16)


def interleave(rows_ref, mean, cat_ref):
    for g in range(8):
        at = slice(g * 128, g * 128 + 128)
        cat_ref[:, g * 256 : g * 256 + 128] = rows_ref[:, at]
        cat_ref[:, g * 256 + 128 : g * 256 + 256] = mean[:, at]


def layer_backward(grad, layer_ref, own_ref, mean_ref):
    for g in range(8):
        at = slice(g * 128, g * 128 + 128)
        both = nt(grad, layer_ref[g * 256 : g * 256 + 256, :])
        own_ref[:, at] = both[:, 0:128]
        mean_ref[:, at] = both[:, 128:256].astype(bf16)


def shard_rows(place_ref, offset):
    return pl.multiple_of(lax.rem(place_ref[1] + offset + 8, 8) * 256, 256)


def lay_layer(place_ref, layer, places, refs, layer_ref, sems):
    copies = []
    for half in range(2):
        side = place_ref[0] if half == 0 else 1 - place_ref[0]
        column = pl.multiple_of(side * 512, 512)
        for index, (array, start, offset) in enumerate(places):
            rows = pl.ds(shard_rows(place_ref, (1 - 2 * side) * offset), 256)
            start += layer * 256
            target = layer_ref.at[rows, pl.ds(column, 512)]
            source = refs[half][array].at[start : start + 256, :]
            copies.append(start_copy(source, target, sems.at[half * 5 + index]))
    return copies


def cotangent_part(place_ref, cot_ref, places, refs, outs):
    own_ref, mean_ref, one_ref, two_ref, one_sems, two_sems = outs
    two_copies = lay_layer(place_ref, 1, places, refs, two_ref, two_sems)
    one_copies = lay_layer(place_ref, 0, places, refs, one_ref, one_sems)
    for copy in two_copies:
        copy.wait()
    for _, _, offset in places:
        rows = shard_rows(place_ref, offset)
        at = pl.ds(pl.multiple_of(lax.rem(place_ref[1] + offset + 8, 8) * 128, 128), 128)
        both = nt(cot_ref[...], two_ref[pl.ds(rows, 256), :])
        own_ref[:, at] = both[:, 0:128]
        mean_ref[:, at] = both[:, 128:256].astype(bf16)
    return one_copies


def cotangent_near(place_ref, cot_ref, mine_ref, theirs_ref, *outs):
    places = [(0, index * 512, layer_order[index]) for index in range(5)]
    for copy in cotangent_part(place_ref, cot_ref, places, ([mine_ref], [theirs_ref]), outs):
        copy.wait()


far_starts = ((0, 2560), (1, 0), (1, 512))


def lay_far(place_ref, cot_ref, half, arrays, one_ref, two_ref):
    side = place_ref[0] if half == 0 else 1 - place_ref[0]
    column = pl.ds(pl.multiple_of(side * 512, 512), 512)
    cot = cot_ref[:, column]
    products = []
    for (array, start), offset in zip(far_starts, layer_order[5:], strict=True):
        rows = pl.ds(shard_rows(place_ref, (1 - 2 * side) * offset), 256)
        one, two = slice(start, start + 256), slice(start + 256, start + 512)
        one_ref[rows, column] = arrays[array][one, :]
        two_ref[rows, column] = arrays[array][two, :]
        products.append(nt(cot, arrays[array][two, :]))
    return products


def cotangent_far_mine(place_ref, cot_ref, near_ref, far_ref, *refs):
    one_ref, two_ref, part_ref = refs[2:]
    products = lay_far(place_ref, cot_ref, 0, (near_ref, far_ref), one_ref, two_ref)
    for index, product in enumerate(products):
        part_ref[:, index * 256 : index * 256 + 256] = product


def cotangent_far_theirs(place_ref, cot_ref, near_ref, far_ref, part_ref, count_t_ref, *refs):
    own_ref, mean_ref, one_ref, two_ref = refs[4:]
    products = lay_far(place_ref, cot_ref, 1, (near_ref, far_ref), one_ref, two_ref)
    for index, offset in enumerate(layer_order[5:]):
        both = part_ref[:, index * 256 : index * 256 + 256] + products[(1, 0, 2)[index]]
        shard = lax.rem(place_ref[1] + (1 - 2 * place_ref[0]) * offset + 8, 8)
        at = pl.ds(pl.multiple_of(shard * 128, 128), 128)
        own_ref[:, at] = both[:, 0:128]
        mean_ref[:, at] = both[:, 128:256].astype(bf16)
    own_ref[...] += nn(count_t_ref[...], mean_ref[...]) / 10.0


def graph_critical(
    in_ref, count_ref, count_t_ref, one_ref, base_ref, grad_ref, out_ref, cat_ref, own_ref, mean_ref
):
    interleave(in_ref, (nn(count_ref[...], in_ref[...]) / 10.0).astype(bf16), cat_ref)
    pre = nn(cat_ref[...], one_ref[...])
    sigmoid = 1.0 / (1.0 + jnp.exp(-pre))
    out_ref[...] = (pre * sigmoid).astype(bf16)
    pre_grad = (base_ref[...] * (sigmoid * (1.0 + pre * (1.0 - sigmoid)))).astype(bf16)
    layer_backward(pre_grad, one_ref, own_ref, mean_ref)
    spread = nn(count_t_ref[...], mean_ref[...]) / 10.0
    grad_ref[...] = (own_ref[...] + spread).astype(bf16)


def graph_output(first_ref, count_ref, two_ref, out_ref, cat_ref):
    interleave(first_ref, (nn(count_ref[...], first_ref[...]) / 10.0).astype(bf16), cat_ref)
    out_ref[...] = nn(cat_ref[...], two_ref[...]).astype(bf16)


def ff_backward(mine_ref, theirs_ref, put_mine_ref, put_theirs_ref, *refs):
    slope_refs, blocks = refs[:2], units(refs[2:-5])
    grad_ref, own_ref, other_ref, both_ref, pre_ref = refs[-5:]
    summed = nn(put_mine_ref[...], mine_ref[...]) + nn(put_theirs_ref[...], theirs_ref[...])
    both_ref[...] = summed.astype(bf16)
    grad_ref[...] = both_ref[0:128, :]
    for pair in range(8):
        late = pair >= early_blocks // 2
        start = pair * 256 - (early_blocks * 128 if late else 0)
        grown = nt(both_ref[...], out_rows(blocks, pair)) * slope_refs[late][:, start : start + 256]
        pre_ref[:, pair * 256 : pair * 256 + 256] = grown.astype(bf16)
    for column in range(0, 1024, 256):
        at = slice(column, column + 256)
        total = nn(pre_ref[:, 0:256], in_rows(blocks, 0, at))
        for pair in range(1, 8):
            total += nn(pre_ref[:, pair * 256 : pair * 256 + 256], in_rows(blocks, pair, at))
        own_ref[:, at] = total[0:128, :]
        other_ref[:, at] = total[128:256, :]


def finish(states_ref, gain_ref, grad_ref, mine_ref, theirs_ref, out_ref, half_ref, sems):
    copies = []
    for half in range(2):
        at = slice(half * 64, half * 64 + 64)
        wide = states_ref[at, :].astype(f32)
        inv_rms = lax.rsqrt(jnp.mean(wide * wide, axis=-1, keepdims=True) + eps_norm)
        scaled = (mine_ref[at, :] + theirs_ref[at, :]) * gain_ref[...]
        cubed = inv_rms * inv_rms * inv_rms
        result = (
            grad_ref[at, :].astype(f32)
            + inv_rms * scaled
            - wide * cubed * jnp.mean(scaled * wide, axis=-1, keepdims=True)
        )
        half_ref[at, :] = result.astype(bf16)
        copies.append(start_copy(half_ref.at[at, :], out_ref.at[at, :], sems.at[half]))
    for copy in copies:
        copy.wait()


def on_device(
    node_states,
    norm_gain,
    w_in,
    w_out,
    self_one,
    neigh_one,
    self_two,
    neigh_two,
    send_slots,
    send_counts,
    neighbors,
    out_cotangent,
):
    gain = norm_gain.reshape(1, 1024)
    block, layer_half, place = local_call(
        prepare,
        [shape_of((256, 1024), bf16), shape_of((512, 512), bf16), shape_of((2,), jnp.int32)],
        "hhhhhh",
        "vvs",
        [pltpu.SemaphoreType.DMA((6,))],
        moved=2 << 20,
        limit=60,
    )(w_in, w_out, self_one, neigh_one, self_two, neigh_two)
    filled = jnp.arange(4, dtype=jnp.int32)[None, :] < send_counts[0][:, None]
    own_ids = jnp.where(filled, send_slots, -1).T
    (packed,) = local_call(pack, [shape_of((144, 1024), bf16)], "vv", "v", moved=1 << 20)(
        node_states, own_ids
    )
    blocks, near_parts, far_parts, other_states = gather_weights(block, layer_half, packed)
    pick_mine, put_mine, put_theirs, count, count_t = local_call(
        index_tables,
        [shape_of((128, 256), bf16)] + [shape_of((256, 128), bf16)] * 2 + [shape_of((128, 128), bf16)] * 2,
        "svvv",
        "vvvvv",
        moved=1 << 20,
    )(place, own_ids, other_states, neighbors.T)

    layer_flops = 2 * 128 * 1024 * 2048
    layer_shapes = [
        shape_of((128, 1024), f32),
        shape_of((128, 1024), bf16),
        shape_of((2048, 1024), bf16),
        shape_of((2048, 1024), bf16),
    ]
    layer_sems = [pltpu.SemaphoreType.DMA((10,))] * 2
    near = local_call(
        cotangent_near, layer_shapes, "svvv", "vvvv", layer_sems, flops=layer_flops // 2, moved=10 << 20
    )(place, out_cotangent, *near_parts)

    far = join_parts(after(far_parts[:2], far_parts, near[1]))
    far_parts = (far, swap(far))

    late_blocks = 16 - early_blocks
    block_flops = 2 * 2 * 256 * 1024 * 128
    early, slope_early, normed = local_call(
        ff_early,
        [
            shape_of((256, 1024), f32),
            shape_of((256, early_blocks * 128), f32),
            shape_of((256, 1024), bf16),
        ],
        "vvv" + "v" * (early_arrays + 1),
        "vvv",
        [pltpu.VMEM((256, early_blocks * 128), bf16)],
        flops=block_flops * early_blocks,
        moved=9 << 20,
    )(node_states, other_states, gain, *blocks[:early_arrays], count_t)
    partial, slope_late = local_call(
        ff_late,
        [shape_of((256, 1024), f32), shape_of((256, late_blocks * 128), f32)],
        "vv" + "v" * (len(blocks) - early_arrays),
        "vv",
        [pltpu.VMEM((256, late_blocks * 128), bf16)],
        flops=block_flops * late_blocks,
        moved=6 << 20,
    )(normed, early, *blocks[early_arrays:])
    partial_theirs = swap(partial)
    near_one, near_two, far_products = local_call(
        cotangent_far_mine,
        [*layer_shapes[2:], shape_of((128, 768), f32)],
        "svvvvv",
        "vvv",
        flops=layer_flops // 5,
        moved=3 << 20,
        aliases={4: 0, 5: 1},
    )(place, out_cotangent, near_parts[0], far_parts[0], *near[2:])
    base, _, layer_one, layer_two = local_call(
        cotangent_far_theirs,
        layer_shapes,
        "svvvvvvvvv",
        "vvvv",
        flops=layer_flops // 5,
        moved=4 << 20,
        aliases={6: 0, 7: 1, 8: 2, 9: 3},
    )(
        place, out_cotangent, near_parts[1], far_parts[1], far_products, count_t,
        near[0], near[1], near_one, near_two,
    )
    (outgoing,) = local_call(
        pick_rows,
        [shape_of((128, 1024), bf16)],
        "vvvvvv",
        "v",
        flops=2 * 128 * 256 * 1024,
        moved=3 << 20,
    )(node_states, other_states, partial, partial_theirs, pick_mine, base)
    incoming = lax.all_to_all(
        outgoing.reshape(16, 8, 1024), ("x", "y"), split_axis=0, concat_axis=0, tiled=True
    ).reshape(128, 1024)
    slot_grad, first_out = local_call(
        graph_critical,
        [shape_of((128, 1024), bf16), shape_of((128, 1024), bf16)],
        "vvvvv",
        "vv",
        [
            pltpu.VMEM((128, 2048), bf16),
            pltpu.VMEM((128, 1024), f32),
            pltpu.VMEM((128, 1024), bf16),
        ],
        flops=2 * layer_flops,
        moved=5 << 20,
    )(incoming, count, count_t, layer_one, base)
    returned = lax.all_to_all(
        slot_grad.reshape(16, 8, 1024), ("x", "y"), split_axis=0, concat_axis=0, tiled=True
    ).reshape(128, 1024)
    returned_theirs = swap(returned)
    embedded_grad, grad_mine, grad_other = local_call(
        ff_backward,
        [shape_of((128, 1024), bf16), shape_of((128, 1024), f32), shape_of((128, 1024), f32)],
        "vvvvvv" + "v" * len(blocks),
        "vvv",
        [pltpu.VMEM((256, 1024), bf16), pltpu.VMEM((256, 2048), bf16)],
        flops=block_flops * 16,
        moved=14 << 20,
    )(returned, returned_theirs, put_mine, put_theirs, slope_early, slope_late, *blocks)
    grad_theirs = swap(grad_other)
    (node_out,) = local_call(
        graph_output,
        [shape_of((128, 1024), bf16)],
        "vvv",
        "b",
        [pltpu.VMEM((128, 2048), bf16)],
        flops=layer_flops,
        moved=5 << 20,
    )(first_out, count, layer_two)
    (state_grad,) = local_call(
        finish,
        [shape_of((128, 1024), bf16)],
        "vvvvv",
        "h",
        [pltpu.VMEM((128, 1024), bf16), pltpu.SemaphoreType.DMA((2,))],
        moved=2 << 20,
    )(node_states, gain, embedded_grad, grad_mine, grad_theirs)
    return node_out, state_grad


def solution(mesh):
    split = Mesh(mesh.devices.reshape(4, 4, 2, 8), ("x", "y", "core", "gnn"))
    lm, everywhere = ("x", "y", "core"), ("x", "y", "core", "gnn")
    rows, by_lm, by_gnn = P(everywhere, None), P(lm, None), P("gnn", None)
    return jax.shard_map(
        on_device,
        mesh=split,
        in_specs=(rows, P(), by_lm, by_lm, by_gnn, by_gnn, by_gnn, by_gnn, rows, rows, rows, rows),
        out_specs=(rows, rows),
        check_vma=False,
    )
```
